32 devices in a mesh: batch: 8 (over z, x), seq: 4 (over y, core).
Axes of the slice: x: 2, y: 2, z: 4, core: 2. Of those that a mesh axis runs over, the one named last changes fastest.
Arguments:
- hidden_in: float32 [32, 512, 768], P('batch', 'seq'), may hold values from -6 to 6
- doc_lengths: int32 [32, 8], P('batch'), may hold values from 1 to 505, as said below
- bias_table: float32 [32, 12], replicated, may hold values from -4 to 4
- gain_attn: bfloat16 [768], P('batch'), may hold values from 0.099609375 to 1.8984375
- gain_ffn: bfloat16 [768], P('batch'), may hold values from 0.099609375 to 1.8984375
- w_query: bfloat16 [768, 768], P('batch'), may hold values from -0.0546875 to 0.0546875
- w_key: bfloat16 [768, 768], P('batch'), may hold values from -0.21875 to 0.21875
- w_value: bfloat16 [768, 768], P('batch'), may hold values from -0.21875 to 0.21875
- w_out: bfloat16 [768, 768], P('batch'), may hold values from -1.25 to 1.25
- w_in: bfloat16 [768, 3072], P('batch'), may hold values from -0.21875 to 0.21875
- w_down: bfloat16 [3072, 768], P('batch'), may hold values from -0.109375 to 0.109375
- out_grad: float32 [32, 512, 768], P('batch', 'seq'), may hold values from -6 to 6
Outputs:
- out_hidden: float32 [32, 512, 768], P('batch', 'seq')
- in_grad: float32 [32, 512, 768], P('batch', 'seq')
- table_grad: float32 [32, 12], replicated
- gain_attn_grad: float32 [768], P(('batch', 'seq'))
- gain_ffn_grad: float32 [768], P(('batch', 'seq'))
- w_query_grad: float32 [768, 768], P(('batch', 'seq'))
- w_key_grad: float32 [768, 768], P(('batch', 'seq'))
- w_value_grad: float32 [768, 768], P(('batch', 'seq'))
- w_out_grad: float32 [768, 768], P(('batch', 'seq'))
- w_in_grad: float32 [768, 3072], P(('batch', 'seq'))
- w_down_grad: float32 [3072, 768], P(('batch', 'seq'))
The draws below stay inside these ranges and needn't reach their ends.
Inputs may be any that keep to these rules, and one draw needn't show every extreme that they name: `doc_lengths`: each row's 8 lengths are positive and sum to 512; in every aligned block of 4 rows one row holds a document of the most length.
All inputs are finite; a program needn't handle non-finite values.
Results may differ from the reference program's by a relative error of at most 0.035.
Values may be sent and summed in bfloat16 or wider, within the bound.
No kernel may reach another device: no remote copies, remote signals or barrier semaphores. Data moves between devices by JAX's collectives and lax.ppermute only.
A program may use at most 192 MiB of HBM per device.

```python
import jax
import jax.numpy as jnp
from jax import lax

D = 768
HEADS = 12
HEAD_DIM = 64
FF = 3072
BUCKETS = 32
ROW_LEN = 512
DOCS = 8
ROWS_DEV = 4
ROWS = 32


def draw_doc_lengths(key, part):
    key = jax.random.fold_in(key, 11)

    def drawn_row(row_key):
        return jnp.sort(jax.random.permutation(row_key, ROW_LEN - 1)[:DOCS - 1] + 1)

    def spanning_row(row_key):
        leading = jax.random.randint(row_key, (), 1, DOCS)
        places = jnp.arange(DOCS - 1)
        return jnp.where(places < leading, places + 1, ROW_LEN - (DOCS - 1 - places))
    drawn_cuts = jax.vmap(drawn_row)(jax.random.split(jax.random.fold_in(key, 1), ROWS))
    span_cuts = jax.vmap(spanning_row)(jax.random.split(jax.random.fold_in(key, 2), ROWS))
    chosen = jax.random.randint(jax.random.fold_in(key, 3), (ROWS // ROWS_DEV,), 0, ROWS_DEV)
    row_index = jnp.arange(ROWS)
    spanning = row_index % ROWS_DEV == chosen[row_index // ROWS_DEV]
    cuts = jnp.where(spanning[:, None], span_cuts, drawn_cuts).astype(jnp.int32)
    starts = jnp.zeros((ROWS, 1), jnp.int32)
    finish = jnp.full((ROWS, 1), ROW_LEN, jnp.int32)
    bounds = jnp.concatenate([starts, cuts, finish], axis=1)
    return (bounds[:, 1:] - bounds[:, :-1]).astype(jnp.int32)


def raised(values, rng, source, target, shards_of, factor):
    def block_of(axis_at):
        return (jnp.arange(values.shape[axis_at]) // (values.shape[axis_at] // shards_of)).reshape((-1,) + (1,) * (values.ndim - 1 - axis_at))

    near = jax.random.permutation(rng, shards_of)[block_of(target)]
    far = (block_of(target) + shards_of // 2) % shards_of
    return jnp.where((block_of(source) == near) | (block_of(source) == far), factor * values, values)


def block_scale(own_key, extent, cuts, low, top_value):
    loudness = 1.0
    for axis_at, parts in cuts:
        steps = jax.random.uniform(jax.random.fold_in(jax.random.fold_in(own_key, 6), axis_at), (parts,), jnp.float32, low / len(cuts), top_value / len(cuts))
        loudness = loudness * jnp.repeat(jnp.exp(steps), extent[axis_at] // parts).reshape((-1,) + (1,) * (len(extent) - 1 - axis_at))
    return loudness


def bell_draw(rng, dims, spread, limit, shards=(), dtype=jnp.bfloat16):
    drawn = jax.random.normal(rng, dims, jnp.float32) * spread
    if len(shards) > 0:
        drawn = block_scale(rng, dims, shards, -0.22, 0.18) * drawn
    return jnp.clip(drawn, min=-limit, max=limit).astype(dtype)


def bell_draw_with(rng, dims, deviation, reach, cuts, heavy, kind=jnp.bfloat16):
    values = deviation * jax.random.normal(rng, dims, jnp.float32)
    if cuts:
        values = values * block_scale(rng, dims, cuts, -0.22, 0.18)
    return jnp.clip(raised(values, jax.random.fold_in(rng, 3), *heavy), -reach, reach).astype(kind)


def setup_inputs(seed: int = 0) -> dict:
    splits = jax.random.split(jax.random.key(seed), 13)
    return {
        "hidden_in": bell_draw_with(splits[0], (ROWS, ROW_LEN, D), 1.0, 6.0, ((0, 8), (1, 4)), (0, 2, 8, 2.0), jnp.float32),
        "doc_lengths": draw_doc_lengths(jax.random.fold_in(splits[12], 71), 0),
        "bias_table": bell_draw(splits[2], (BUCKETS, HEADS), 1.0, 4.0, (), jnp.float32),
        "gain_attn": jnp.clip(1.0 + 0.18 * jax.random.normal(splits[3], (D,), jnp.float32), 0.099609375, 1.8984375).astype(jnp.bfloat16),
        "gain_ffn": jnp.clip(1.0 + 0.18 * jax.random.normal(splits[4], (D,), jnp.float32), 0.099609375, 1.8984375).astype(jnp.bfloat16),
        "w_query": bell_draw(splits[5], (D, D), (D * HEAD_DIM // 4) ** -0.5, 0.0546875, ((0, 8),)),
        "w_key": bell_draw(splits[6], (D, D), D ** -0.5, 0.21875, ((0, 8),)),
        "w_value": bell_draw(splits[7], (D, D), D ** -0.5, 0.21875, ((0, 8),)),
        "w_out": bell_draw(splits[8], (D, D), (D // 32) ** -0.5, 1.25, ((0, 8),)),
        "w_in": bell_draw(splits[9], (D, FF), D ** -0.5, 0.21875, ((0, 8),)),
        "w_down": bell_draw(splits[10], (FF, D), FF ** -0.5, 0.109375, ((0, 8),)),
        "out_grad": bell_draw(splits[11], (ROWS, ROW_LEN, D), 1.0, 6.0, ((0, 8), (1, 4)), jnp.float32),
    }


EPS = 1e-06
THRESHOLDS = (12, 16, 23, 32, 46, 64, 91)
HIGHEST = lax.Precision.HIGHEST

@jax.custom_vjp
def low(v):
    return lax.optimization_barrier(v.astype(jnp.bfloat16)).astype(jnp.float32)

@jax.custom_vjp
def low_back(v):
    return v

def low_keep(v):
    return (low(v), None)

def low_pass(kept, grad):
    return (grad,)

def back_keep(v):
    return (v, None)

def back_low(kept, grad):
    return (low(grad),)
low.defvjp(low_keep, low_pass)
low_back.defvjp(back_keep, back_low)

def bucket_of(offsets):
    distance = jnp.abs(offsets)
    stepped = jnp.full_like(distance, 8)
    for threshold in THRESHOLDS:
        stepped = stepped + (distance >= threshold).astype(jnp.int32)
    closer = jnp.where(distance < 8, distance, stepped)
    return (closer + 16 * (offsets > 0).astype(jnp.int32)).astype(jnp.int32)

def segments_of(lengths, places):
    ends = jnp.cumsum(lengths, axis=-1).astype(jnp.int32)
    return lax.optimization_barrier(jnp.sum((places[None, :, None] >= ends[:, None, :]).astype(jnp.int32), axis=-1)).astype(jnp.int32)

def rms_norm(values, gain):
    return values * lax.rsqrt(lax.optimization_barrier(jnp.mean(values * values, axis=-1, keepdims=True)) + EPS) * gain

def matmul(left, right):
    return jnp.dot(left, right, precision=HIGHEST, preferred_element_type=jnp.float32)

def layer(hidden, lengths, bias_rows, gain_one, gain_two, w_query, w_key, w_value, w_out, w_in, w_down):
    row_count = hidden.shape[0]
    places = jnp.arange(ROW_LEN).astype(jnp.int32)
    segment = segments_of(lengths, places)
    allowed = segment[:, None, :, None] == segment[:, None, None, :]
    buckets = bucket_of(places[None, :] - places[:, None])
    rel_bias = jnp.transpose(bias_rows[buckets], (2, 0, 1))
    normed = low(rms_norm(hidden, gain_one))

    def project(weight):
        return low_back(low(matmul(normed, weight))).reshape(row_count, ROW_LEN, HEADS, HEAD_DIM)
    queries = project(w_query)
    keys_all = project(w_key)
    values = project(w_value)
    scores = jnp.einsum('gqhd,gkhd->ghqk', queries, keys_all, precision=HIGHEST) + rel_bias[None]
    scores = jnp.where(allowed, low_back(scores), -1e+30)
    largest = lax.optimization_barrier(jnp.max(scores, axis=-1, keepdims=True))
    exponent = jnp.exp(scores - largest)
    probabilities = exponent / lax.optimization_barrier(jnp.sum(exponent, axis=-1, keepdims=True))
    context = jnp.einsum('ghqk,gkhd->gqhd', low(probabilities), values, precision=HIGHEST)
    context = low_back(low(context)).reshape(row_count, ROW_LEN, D)
    middle = hidden + low_back(matmul(context, w_out))
    second = low(rms_norm(middle, gain_two))
    upward = low_back(matmul(second, w_in))
    active = low(jax.nn.gelu(upward, approximate=False))
    return middle + low_back(matmul(active, w_down))

def reference(hidden_in, doc_lengths, bias_table, gain_attn, gain_ffn, w_query, w_key, w_value, w_out, w_in, w_down, out_grad):
    group_rows = 8
    blocks = ROWS // group_rows
    inputs = hidden_in.astype(jnp.float32).reshape(blocks, group_rows, ROW_LEN, D)
    lengths = doc_lengths.reshape(blocks, group_rows, DOCS)
    params = tuple((member.astype(jnp.float32) for member in (bias_table, gain_attn, gain_ffn, w_query, w_key, w_value, w_out, w_in, w_down)))
    checked = jax.checkpoint(layer)

    def forward(states, *weights):

        def visiting(pieces):
            return checked(pieces[0], pieces[1], *weights)
        return lax.map(visiting, (states, lengths))
    outputs, backward = jax.vjp(forward, inputs, *params)
    gradients = backward(out_grad.astype(jnp.float32).reshape(blocks, group_rows, ROW_LEN, D))
    return (outputs.reshape(ROWS, ROW_LEN, D), gradients[0].reshape(ROWS, ROW_LEN, D), gradients[1], gradients[2], gradients[3], gradients[4], gradients[5], gradients[6], gradients[7], gradients[8], gradients[9])
```

```python
import functools

import jax
import jax.numpy as jnp
from jax import lax
from jax.experimental import pallas as pl
from jax.experimental.pallas import tpu as pltpu
from jax.sharding import PartitionSpec as P

HEADS = 12
HEAD_DIM = 64
BUCKETS = 32
TILE = 128

EPS = 1e-06
THRESHOLDS = (12, 16, 23, 32, 46, 64, 91)
HIGHEST = lax.Precision.HIGHEST
F32 = jnp.float32
BF16 = jnp.bfloat16
VMEM_LIMIT = 56 * 1024 * 1024


def bucket_of(offsets):
    distance = jnp.abs(offsets)
    stepped = jnp.full_like(distance, 8)
    for threshold in THRESHOLDS:
        stepped = stepped + (distance >= threshold).astype(jnp.int32)
    closer = jnp.where(distance < 8, distance, stepped)
    return closer + 16 * (offsets > 0).astype(jnp.int32)


def nn(left, right):
    return lax.dot_general(left, right, (((1,), (0,)), ((), ())), preferred_element_type=F32)


def nt(left, right):
    return lax.dot_general(left, right, (((1,), (1,)), ((), ())), preferred_element_type=F32)


def tn(left, right):
    return lax.dot_general(left, right, (((0,), (0,)), ((), ())), preferred_element_type=F32)


def params(**kw):
    return pltpu.CompilerParams(vmem_limit_bytes=VMEM_LIMIT, **kw)


def fill(where, parts, out):
    own, far, own_c, far_c = parts
    b, s = where[0], where[1]
    c = s % 2
    for x in range(2):
        for z in range(own.shape[1]):
            t = (2 * z + x) ^ b
            out[t, c] = own[x, z, 0]
            out[t, 1 - c] = own_c[x, z, 0]
            out[t, 2 + s] = own[x, z, 1]
            out[t, 2 + (s ^ 1)] = own_c[x, z, 1]
            out[t, 2 + (s ^ 2)] = far[x, z]
            out[t, 2 + (s ^ 3)] = far_c[x, z]


def flat(ref, columns=None):
    value = ref[...] if columns is None else ref[:, :, :, columns]
    return value.reshape(-1, value.shape[-1])


def weight_kernel(where, own, far, own_c, far_c, out_ref):
    fill(where, (own, far, own_c, far_c), out_ref)


def qkv_kernel(x_ref, gain_ref, w_ref, perm_ref, qkv_ref, first_t_ref):
    x = x_ref[...].astype(F32)
    r1 = lax.rsqrt(jnp.mean(x * x, axis=-1, keepdims=True) + EPS)
    first = (x * r1 * gain_ref[...]).astype(BF16)
    qkv_ref[...] = nn(first, w_ref[...]).astype(BF16)
    first_t_ref[...] = nt(perm_ref[...], first).astype(BF16)


def attention_kernel(q_ref, k_ref, v_ref, band_ref, table_ref, segc_ref, segr_ref, probs_ref, ctx_ref):
    pair = pl.program_id(0)
    length = q_ref.shape[0]
    tiles = length // TILE
    q, k, v = q_ref[...], k_ref[...], v_ref[...]
    lane = lax.broadcasted_iota(jnp.int32, (TILE, TILE), 1)
    keys_seg = segr_ref[...]
    for t in range(tiles):
        rows = slice(t * TILE, (t + 1) * TILE)
        allowed = segc_ref[rows, :] == keys_seg
        halves = []
        for h in range(2):
            mine = (lane < HEAD_DIM) if h == 0 else (lane >= HEAD_DIM)
            qh = jnp.where(mine, q[rows], jnp.zeros_like(q[rows]))
            s = nt(qh, k)
            below = table_ref[15, 2 * pair + h]
            above = table_ref[31, 2 * pair + h]
            parts = []
            for u in range(tiles):
                d = u - t
                part = s[:, u * TILE : (u + 1) * TILE]
                if abs(d) <= 1:
                    part = part + band_ref[h, :, (d + 1) * TILE : (d + 2) * TILE]
                else:
                    part = part + (above if d > 0 else below)
                parts.append(part)
            s = jnp.where(allowed, jnp.concatenate(parts, axis=1), -1e30)
            p = jnp.exp(s - jnp.max(s, axis=-1, keepdims=True))
            p = (p * (1.0 / jnp.sum(p, axis=-1, keepdims=True))).astype(BF16)
            probs_ref[h, rows, :] = p
            halves.append(nn(p, v))
        ctx_ref[rows, :] = jnp.where(lane < HEAD_DIM, halves[0], halves[1]).astype(BF16)


def out_kernel(x_ref, ctx_ref, w_ref, gain_ref, perm_ref, attn_ref, second_ref, second_t_ref):
    attn = nn(ctx_ref[...], w_ref[...])
    attn_ref[...] = attn
    middle = x_ref[...].astype(F32) + attn
    r2 = lax.rsqrt(jnp.mean(middle * middle, axis=-1, keepdims=True) + EPS)
    second = (middle * r2 * gain_ref[...]).astype(BF16)
    second_ref[...] = second
    second_t_ref[...] = nt(perm_ref[...], second).astype(BF16)


def ffn_kernel(
    place, second_ref, second_t_ref, glow_ref, attn_ref, win_ref, wd_ref,
    delta_ref, dsec_ref, win_keep_ref, win_send_ref, wd_keep_ref, wd_send_ref, acc_ref, dacc_ref,
):
    j = pl.program_id(0)
    glow = glow_ref[...]
    win, wd = win_ref[...], wd_ref[...]
    up = nn(second_ref[...], win)
    phi_cap = 0.5 * (1.0 + lax.erf(up * 0.7071067811865476))
    act = (up * phi_cap).astype(BF16)
    slope = phi_cap + up * (jnp.exp(-0.5 * up * up) * 0.3989422804014327)
    gup = (nt(glow, wd) * slope).astype(BF16)
    out = nn(act, wd)
    dsec = nt(gup, win)

    @pl.when(j == 0)
    def _():
        acc_ref[...] = attn_ref[...] + out
        dacc_ref[...] = dsec

    @pl.when(j > 0)
    def _():
        acc_ref[...] += out
        dacc_ref[...] += dsec

    @pl.when(j == pl.num_programs(0) - 1)
    def _():
        delta_ref[...] = acc_ref[...].astype(BF16)
        dsec_ref[...] = dacc_ref[...]

    dwin = nn(second_t_ref[...], gup).astype(BF16)
    half = dwin.shape[0] // 2
    win_keep_ref[...] = dwin[:half]
    win_send_ref[...] = dwin[half:]
    dwd = tn(act, glow)
    if len(wd_keep_ref.shape) == 2:
        wd_keep_ref[...] = dwd.astype(BF16)
    else:
        rows = wd_keep_ref.shape[-2]
        blocks = [dwd[i * rows : (i + 1) * rows].astype(BF16) for i in range(8)]
        for axis, bit in ((1, 4), (2, 2), (3, 1)):
            flip = place[axis] == 1
            blocks = [jnp.where(flip, blocks[i ^ bit], blocks[i]) for i in range(8)]
        for x in range(2):
            for y in range(2):
                wd_keep_ref[y, x, 0] = blocks[4 * x + 2 * y]
                wd_send_ref[y, x, 0] = blocks[4 * x + 2 * y + 1]


def mid_kernel(
    x_ref, attn_ref, gain_ref, dsec_ref, glow_ref, ctx_ref, perm_ref, w_ref,
    gmd_ref, g2_ref, dctx_ref, keep_ref, send_ref,
):
    middle = x_ref[...].astype(F32) + attn_ref[...]
    r2 = lax.rsqrt(jnp.mean(middle * middle, axis=-1, keepdims=True) + EPS)
    normed = middle * r2
    dsec = dsec_ref[...]
    g2_ref[...] = jnp.sum(dsec * normed, axis=0, keepdims=True)
    scaled = dsec * gain_ref[...]
    gmd = r2 * (scaled - normed * jnp.mean(scaled * normed, axis=-1, keepdims=True))
    gmd_ref[...] = gmd
    low = (glow_ref[...].astype(F32) + gmd).astype(BF16)
    dctx_ref[...] = nt(low, w_ref[...]).astype(BF16)
    ctx_t = nt(perm_ref[...], ctx_ref[...]).astype(BF16)
    dw = nn(ctx_t, low).astype(BF16)
    half = dw.shape[0] // 2
    keep_ref[...] = dw[:half]
    send_ref[...] = dw[half:]


def back_kernel(q_ref, k_ref, v_ref, dctx_ref, ctx_ref, probs_ref, dq_ref, dk_ref, dv_ref, band_ref, far_ref, ds_ref):
    length = q_ref.shape[0]
    tiles = length // TILE
    q, k, v, dctx = q_ref[...], k_ref[...], v_ref[...], dctx_ref[...]
    lane = lax.broadcasted_iota(jnp.int32, (length, TILE), 1)
    product = dctx.astype(F32) * ctx_ref[...].astype(F32)
    dqs, dk, dv = [], None, None
    for h in range(2):
        mine = (lane < HEAD_DIM) if h == 0 else (lane >= HEAD_DIM)
        do = jnp.where(mine, dctx, jnp.zeros_like(dctx))
        qh = jnp.where(mine, q, jnp.zeros_like(q))
        delta = jnp.sum(jnp.where(mine, product, 0.0), axis=-1, keepdims=True)
        band = [None, None, None]
        far = [None, None]

        def put(old, new):
            return new if old is None else old + new

        for t in range(tiles):
            rows = slice(t * TILE, (t + 1) * TILE)
            dp = nt(do[rows], v)
            ds = probs_ref[h, rows, :].astype(F32) * (dp - delta[rows])
            ds_ref[h, rows, :] = ds.astype(BF16)
            for u in range(tiles):
                d = u - t
                part = ds[:, u * TILE : (u + 1) * TILE]
                if abs(d) <= 1:
                    band[d + 1] = put(band[d + 1], part)
                else:
                    far[int(d > 0)] = put(far[int(d > 0)], part)
        for i in range(3):
            band_ref[h, :, i * TILE : (i + 1) * TILE] = band[i]
        for i in range(2):
            far_ref[h, i : i + 1, :] = jnp.sum(far[i], axis=0, keepdims=True)
        dqs.append(nn(ds_ref[h], k))
        dk_h = tn(ds_ref[h], qh)
        dv_h = tn(probs_ref[h], do)
        dk = dk_h if dk is None else dk + dk_h
        dv = dv_h if dv is None else dv + dv_h
    dq_ref[...] = jnp.where(lane < HEAD_DIM, dqs[0], dqs[1]).astype(BF16)
    dk_ref[...] = dk.astype(BF16)
    dv_ref[...] = dv.astype(BF16)


def first_kernel(
    x_ref, gain_ref, dq_ref, dk_ref, dv_ref, w_ref, first_t_ref, perm_ref, gmd_ref, g2_ref, extra_ref,
    delta_ref, keep1_ref, send1_ref, keep2_ref, send2_ref,
):
    width = x_ref.shape[1]
    x = x_ref[...].astype(F32)
    r1 = lax.rsqrt(jnp.mean(x * x, axis=-1, keepdims=True) + EPS)
    normed = x * r1
    grads = jnp.concatenate([dq_ref[...], dk_ref[...], dv_ref[...]], axis=1)
    dfirst = nt(grads, w_ref[...])
    g1 = jnp.sum(dfirst * normed, axis=0, keepdims=True)
    scaled = dfirst * gain_ref[...]
    delta = gmd_ref[...] + r1 * (scaled - normed * jnp.mean(scaled * normed, axis=-1, keepdims=True))
    delta_ref[...] = delta.astype(BF16)
    dw = nn(first_t_ref[...], grads).astype(BF16)
    row = lax.broadcasted_iota(jnp.int32, (extra_ref.shape[1], width), 0)
    both = jnp.where(row == 0, g1, jnp.where(row == 1, g2_ref[...], 0.0)).astype(BF16)
    extra = (nt(perm_ref[...], both) + extra_ref[...]).astype(BF16)
    half = dw.shape[0] // 2
    split = keep1_ref.shape[1]
    keep1_ref[...] = dw[:half, :split]
    send1_ref[...] = dw[half:, :split]
    rest = dw.shape[1] - split
    keep2_ref[:, :rest] = dw[:half, split:]
    send2_ref[:, :rest] = dw[half:, split:]
    keep2_ref[:, rest:] = extra[:half]
    send2_ref[:, rest:] = extra[half:]


def shape(dims, dtype):
    return jax.ShapeDtypeStruct(tuple(dims), dtype)


def add(left, right):
    return (left.astype(F32) + right.astype(F32)).astype(BF16)


def on_device(
    nb, ns, hidden_in, doc_lengths, bias_table, gain_attn, gain_ffn,
    w_query, w_key, w_value, w_out, w_in, w_down, out_grad,
):
    rows_dev, shard_len, width = hidden_in.shape
    length = ns * shard_len
    ff = w_in.shape[1]
    nz = nb // 2
    b, s = lax.axis_index("batch"), lax.axis_index("seq")
    y, c = s // 2, s % 2
    sizes = {"batch": nb, "seq": ns}
    where = jnp.stack([b, s]).astype(jnp.int32)

    def swap(value, axis, mask):
        return lax.ppermute(value, axis, [(i, i ^ mask) for i in range(sizes[axis])])

    def xor_order(value):
        value = value.reshape((2, 2) + value.shape[1:])
        value = jnp.where(y == 1, value[::-1], value)
        value = jnp.where(c == 1, value[:, ::-1], value)
        return value.reshape((4,) + value.shape[2:])

    def exchange(value):
        value = value.reshape((2, 2) + value.shape[1:])
        mine = lax.dynamic_index_in_dim(value, y, 0, keepdims=False)
        theirs = lax.dynamic_index_in_dim(value, 1 - y, 0, keepdims=False)
        both = jnp.stack([mine, swap(theirs, "seq", 2)])
        kept = lax.dynamic_index_in_dim(both, c, 1, keepdims=False)
        given = lax.dynamic_index_in_dim(both, 1 - c, 1, keepdims=False)
        got = swap(given, "seq", 1)
        return xor_order(jnp.stack([kept[0], got[0], kept[1], got[1]]))

    def gather(shard):
        unit = shard.shape[0] // 6
        common = lax.dynamic_slice_in_dim(shard, c * unit, unit, 0)
        quarter = lax.dynamic_slice_in_dim(shard, (2 + s) * unit, unit, 0)
        block = jnp.stack([common, quarter])[None]
        if nz <= 4:
            block = jnp.concatenate([block] + [swap(block, "batch", 2 * k) for k in range(1, nz)])
        else:
            k = 1
            while k < nz:
                block = jnp.concatenate([block, swap(block, "batch", 2 * k)])
                k *= 2
        own = jnp.stack([block, swap(block, "batch", 1)])
        far = swap(own[:, :, 1], "seq", 2)
        return own, far, swap(own, "seq", 1), swap(far, "seq", 1)

    def assemble(parts):
        own, far, own_c, far_c = parts
        unit, columns = own.shape[-2:]
        if unit % 16 == 0:
            full = pl.pallas_call(
                weight_kernel,
                out_shape=shape((nb, 6, unit, columns), BF16),
                in_specs=[pl.BlockSpec(memory_space=pltpu.SMEM)] + [pl.BlockSpec(memory_space=pltpu.VMEM)] * 4,
                compiler_params=params(),
            )(where, own, far, own_c, far_c)
        else:
            rel = jnp.arange(nb) ^ b
            xi, zi = (rel % 2)[None], (rel // 2)[None]
            common = jnp.stack([own[:, :, 0], own_c[:, :, 0]])
            quarter = jnp.stack([own[:, :, 1], own_c[:, :, 1], far, far_c])
            common = common[(jnp.arange(2) ^ c)[:, None], xi, zi]
            quarter = quarter[(jnp.arange(4) ^ s)[:, None], xi, zi]
            full = jnp.swapaxes(jnp.concatenate([common, quarter]), 0, 1)
        return full.reshape(nb * 6 * unit, columns)

    def scatter(keep, send, x_first):
        value = add(keep, swap(send, "seq", 1))
        if x_first:
            value = add(value[:, 0], swap(value[:, 1], "batch", 1))
            value = add(value[0], swap(value[1], "seq", 2))
        else:
            value = add(value[0], swap(value[1], "seq", 2))
            value = add(value[0], swap(value[1], "batch", 1))
        if nz == 4:
            got = [value[0]] + [swap(value[k], "batch", 2 * k) for k in (1, 2, 3)]
            got = [part.astype(F32) for part in got]
            return (got[0] + got[1]) + (got[2] + got[3])
        half = nz // 2
        while half:
            value = value[:half].astype(F32) + swap(value[half:], "batch", 2 * half).astype(F32)
            value = value.astype(BF16) if half > 1 else value
            half //= 2
        return value[0]

    gains = jnp.stack([gain_attn, gain_ffn])
    shard = w_query.shape[0]
    gains = jnp.tile(gains, (shard // 2, 1))
    gains = jnp.pad(gains, ((0, 0), (0, TILE - shard)))
    packet1 = gather(jnp.concatenate([w_query, w_key, w_value, gains], axis=1))
    packed = jnp.stack([hidden_in.astype(BF16), out_grad.astype(BF16)], axis=1)
    rows = exchange(packed)
    xb = rows[:, 0].reshape(length, width)
    glow = rows[:, 1].reshape(length, width)
    packet2 = gather(jnp.concatenate([w_out, w_in], axis=1))
    packet3 = gather(w_down)

    ends = jnp.cumsum(lax.dynamic_index_in_dim(doc_lengths, s, 0, keepdims=False))
    segments = jnp.sum((jnp.arange(length)[:, None] >= ends[None, :]).astype(jnp.int32), axis=-1)
    seg_column, seg_row = segments.reshape(length, 1), segments.reshape(1, length)
    offsets = jnp.arange(3 * TILE)[None, :] - TILE - jnp.arange(TILE)[:, None]
    buckets = bucket_of(offsets).reshape(1, -1)
    indicator = (jnp.arange(BUCKETS)[:, None] == buckets).astype(F32)
    band = jnp.dot(bias_table.T, indicator, precision=HIGHEST).reshape(HEADS, TILE, 3 * TILE)

    per = width // (nb * ns)
    feature = jnp.arange(width)
    fb, fs, fr = feature // (per * ns) ^ b, feature // per % ns ^ s, feature % per
    position = ((((fs % 2) * 2 + fs // 2) * 2 + fb % 2) * nz + fb // 2) * per + fr
    perm = (jnp.arange(width)[:, None] == position[None, :]).astype(BF16)

    w1 = assemble(packet1)
    gain_rows = w1.reshape(nb, shard, -1)[:, :2, 3 * width : 3 * width + shard].astype(F32)
    gain_one = gain_rows[:, 0].reshape(1, width)
    gain_two = gain_rows[:, 1].reshape(1, width)
    w1 = w1[:, : 3 * width]

    qkv, first_t = pl.pallas_call(
        qkv_kernel,
        out_shape=(shape((length, 3 * width), BF16), shape((width, length), BF16)),
        compiler_params=params(),
    )(xb, gain_one, w1, perm)

    pairs = HEADS // 2
    pair_block = lambda first: pl.BlockSpec((length, TILE), lambda p: (0, first + p))
    head_block = lambda *dims: pl.BlockSpec((2,) + dims, lambda p: (p,) + (0,) * len(dims))
    whole_block = lambda *dims: pl.BlockSpec(dims, lambda p: (0,) * len(dims))
    smem = pl.BlockSpec(memory_space=pltpu.SMEM)
    probs, ctx = pl.pallas_call(
        attention_kernel,
        grid=(pairs,),
        out_shape=(shape((HEADS, length, length), BF16), shape((length, width), BF16)),
        in_specs=[
            pair_block(0), pair_block(pairs), pair_block(2 * pairs), head_block(TILE, 3 * TILE), smem,
            whole_block(length, 1), whole_block(1, length),
        ],
        out_specs=(head_block(length, length), pair_block(0)),
        compiler_params=params(),
    )(qkv, qkv, qkv, band, bias_table, seg_column, seg_row)

    w2 = assemble(packet2)
    w_out_full, w_in_full = w2[:, :width], w2[:, width:]
    attn, second, second_t = pl.pallas_call(
        out_kernel,
        out_shape=(shape((length, width), F32), shape((length, width), BF16), shape((width, length), BF16)),
        compiler_params=params(),
    )(xb, ctx, w_out_full, gain_two, perm)

    wd = assemble(packet3)
    steps = 4
    part = ff // steps
    per_down = ff // (nb * ns)
    aligned = nz == steps and per_down % 16 == 0
    if aligned:
        wd_block = pl.BlockSpec((2, 2, 1, per_down, width), lambda j, place: (0, 0, j ^ place[0], 0, 0))
        wd_shape = shape((2, 2, nz, per_down, width), BF16)
        wd_shapes, wd_blocks = (wd_shape, wd_shape), (wd_block, wd_block)
    else:
        wd_shapes = (shape((ff, width), BF16), shape((8, TILE), BF16))
        wd_blocks = (
            pl.BlockSpec((part, width), lambda j, place: (j, 0)),
            pl.BlockSpec((8, TILE), lambda j, place: (0, 0)),
        )
    place = jnp.stack([b // 2, b % 2, y, c]).astype(jnp.int32)
    full = lambda *dims: pl.BlockSpec(dims, lambda j, place: (0,) * len(dims))
    half = width // 2
    column_block = lambda r: pl.BlockSpec((r, part), lambda j, place: (0, j))
    delta, dsec, win_keep, win_send, wd_keep, wd_send = pl.pallas_call(
        ffn_kernel,
        out_shape=(
            shape((length, width), BF16), shape((length, width), F32),
            shape((half, ff), BF16), shape((half, ff), BF16), *wd_shapes,
        ),
        grid_spec=pltpu.PrefetchScalarGridSpec(
            num_scalar_prefetch=1,
            grid=(steps,),
            in_specs=[
                full(length, width), full(width, length), full(length, width), full(length, width),
                column_block(width), pl.BlockSpec((part, width), lambda j, place: (j, 0)),
            ],
            out_specs=(full(length, width), full(length, width), column_block(half), column_block(half), *wd_blocks),
            scratch_shapes=[pltpu.VMEM((length, width), F32), pltpu.VMEM((length, width), F32)],
        ),
        compiler_params=params(),
    )(place, second, second_t, glow, attn, w_in_full, wd)

    rel = lambda value: value.reshape(2, 2, nz, per, value.shape[-1])
    if not aligned:
        blocks = wd_keep.reshape(nz, 2, 2, 2, per_down, width)
        zi = (jnp.arange(nz) ^ (b // 2))[None, None, :]
        xi = (jnp.arange(2) ^ (b % 2))[None, :, None]
        yi = (jnp.arange(2) ^ y)[:, None, None]
        wd_keep, wd_send = blocks[zi, xi, yi, c], blocks[zi, xi, yi, 1 - c]
    in_grad_w = scatter(rel(win_keep), rel(win_send), False)
    down_grad_w = scatter(wd_keep, wd_send, True)

    gmd, g2, dctx, wo_keep, wo_send = pl.pallas_call(
        mid_kernel,
        out_shape=(
            shape((length, width), F32), shape((1, width), F32), shape((length, width), BF16),
            shape((half, width), BF16), shape((half, width), BF16),
        ),
        compiler_params=params(),
    )(xb, attn, gain_two, dsec, glow, ctx, perm, w_out_full)
    out_grad_w = scatter(rel(wo_keep), rel(wo_send), False)

    dq, dk, dv, dband, dfar = pl.pallas_call(
        back_kernel,
        grid=(pairs,),
        out_shape=(
            *(shape((length, width), BF16),) * 3, shape((HEADS, TILE, 3 * TILE), F32), shape((HEADS, 2, TILE), F32),
        ),
        in_specs=[
            pair_block(0), pair_block(pairs), pair_block(2 * pairs), pair_block(0), pair_block(0),
            head_block(length, length),
        ],
        out_specs=(pair_block(0), pair_block(0), pair_block(0), head_block(TILE, 3 * TILE), head_block(2, TILE)),
        scratch_shapes=[pltpu.VMEM((2, length, length), BF16)],
        compiler_params=params(),
    )(qkv, qkv, qkv, dctx, ctx, probs)

    table = jnp.dot(indicator, dband.reshape(HEADS, -1).T, precision=HIGHEST)
    far_sums = jnp.sum(dfar, axis=-1)
    bucket_row = jnp.arange(BUCKETS)[:, None]
    table = table + jnp.where(bucket_row == 15, far_sums[:, 0], jnp.where(bucket_row == 31, far_sums[:, 1], 0.0))
    table_size = BUCKETS * HEADS
    spare = -(-table_size // per)
    extra_width = -(-(2 + spare) // TILE) * TILE
    flat = jnp.pad(table.reshape(-1), (0, spare * per - table_size)).reshape(per, spare)
    extra = jnp.pad(jnp.tile(flat, (nb * ns, 1)), ((0, 0), (2, extra_width - 2 - spare)))

    split = 3 * width // 2
    in_delta, keep1, send1, keep2, send2 = pl.pallas_call(
        first_kernel,
        out_shape=(
            shape((length, width), BF16),
            *(shape((half, split), BF16),) * 2, *(shape((half, 3 * width - split + extra_width), BF16),) * 2,
        ),
        compiler_params=params(),
    )(xb, gain_one, dq, dk, dv, w1, first_t, perm, gmd, g2, extra)
    part1 = scatter(rel(keep1), rel(send1), False)
    part2 = scatter(rel(keep2), rel(send2), True)
    summed = jnp.concatenate([part1, part2], axis=1)
    tail = summed[:, 3 * width :]
    table_grad = tail[:, 2 : 2 + spare].reshape(-1)[:table_size].reshape(BUCKETS, HEADS)

    out_hidden = hidden_in + exchange(delta.reshape(4, shard_len, width)).astype(F32)
    input_grad = out_grad + exchange(in_delta.reshape(4, shard_len, width)).astype(F32)
    return (
        out_hidden,
        input_grad,
        table_grad,
        tail[:, 0],
        tail[:, 1],
        summed[:, :width],
        summed[:, width : 2 * width],
        summed[:, 2 * width : 3 * width],
        out_grad_w,
        in_grad_w,
        down_grad_w,
    )


def solution(mesh):
    nb, ns = mesh.shape["batch"], mesh.shape["seq"]
    placed = (
        P("batch", "seq", None),
        P("batch", None),
        P(),
        P("batch"),
        P("batch"),
        P("batch", None),
        P("batch", None),
        P("batch", None),
        P("batch", None),
        P("batch", None),
        P("batch", None),
        P("batch", "seq", None),
    )
    both = ("batch", "seq")
    return jax.shard_map(
        functools.partial(on_device, nb, ns),
        mesh=mesh,
        in_specs=placed,
        out_specs=(
            P("batch", "seq", None),
            P("batch", "seq", None),
            P(),
            P(both),
            P(both),
            P(both, None),
            P(both, None),
            P(both, None),
            P(both, None),
            P(both, None),
            P(both, None),
        ),
        check_vma=False,
    )
```

```python
import functools

import jax
import jax.numpy as jnp
from jax import lax
from jax.experimental import pallas as pl
from jax.experimental.pallas import tpu as pltpu
from jax.sharding import PartitionSpec as P

HEADS = 12
HEAD_DIM = 64
BUCKETS = 32
TILE = 128

EPS = 1e-06
THRESHOLDS = (12, 16, 23, 32, 46, 64, 91)
HIGHEST = lax.Precision.HIGHEST
F32 = jnp.float32
BF16 = jnp.bfloat16
VMEM_LIMIT = 56 * 1024 * 1024


def bucket_of(offsets):
    distance = jnp.abs(offsets)
    stepped = jnp.full_like(distance, 8)
    for threshold in THRESHOLDS:
        stepped = stepped + (distance >= threshold).astype(jnp.int32)
    closer = jnp.where(distance < 8, distance, stepped)
    return closer + 16 * (offsets > 0).astype(jnp.int32)


def nn(left, right):
    return lax.dot_general(left, right, (((1,), (0,)), ((), ())), preferred_element_type=F32)


def nt(left, right):
    return lax.dot_general(left, right, (((1,), (1,)), ((), ())), preferred_element_type=F32)


def tn(left, right):
    return lax.dot_general(left, right, (((0,), (0,)), ((), ())), preferred_element_type=F32)


def params(**kw):
    return pltpu.CompilerParams(vmem_limit_bytes=VMEM_LIMIT, **kw)


def cost(microseconds):
    return pl.CostEstimate(flops=int(microseconds * 1e9), bytes_accessed=int(microseconds * 3.5e6), transcendentals=0)


def pack_kernel(where, hidden_ref, grad_ref, keep_ref, mate_ref, away_ref):
    for rel in range(4):
        row = where[1] ^ rel
        target = (keep_ref, mate_ref, away_ref.at[0], away_ref.at[1])[rel]
        target[0] = hidden_ref[row].astype(BF16)
        target[1] = grad_ref[row].astype(BF16)


def unpack_kernel(where, old_ref, keep_ref, mate_ref, away_ref, far_ref, new_ref):
    for rel in range(4):
        row = where[1] ^ rel
        source = (keep_ref[...], mate_ref[...], away_ref[0], far_ref[...])[rel]
        new_ref[row] = old_ref[row] + source.astype(F32)


def place_rows(where, value, keep_ref, mate_ref, away_ref, hold_ref):
    size = keep_ref.shape[0]
    hold_ref[...] = value.astype(BF16).reshape(4, size, value.shape[1])
    for rel in range(4):
        target = (keep_ref, mate_ref, away_ref.at[0], away_ref.at[1])[rel]
        target[...] = hold_ref[where[1] ^ rel]


def fill(where, pieces, out, rows_last):
    b, s = where[0], where[1]
    parts, shards = (out.shape[1], out.shape[0]) if rows_last else (out.shape[0], out.shape[1])
    for ref, flip, base in pieces:
        core = (s ^ flip) % 2
        part = (s ^ flip) if parts == 4 else core
        for i in range(ref.shape[0]):
            t = b ^ where[2 + core * shards + base + i]
            if rows_last:
                out[t, part] = ref[i]
            else:
                out[part, t] = ref[i]


def flat(ref):
    return ref[...].reshape(-1, ref.shape[-1])


def weight_kernel(pattern, rows_last, where, *refs):
    fill(where, [(ref, *entry) for ref, entry in zip(refs, pattern)], refs[-1], rows_last)


def columns_of(w_ref, start, stop):
    size = w_ref.shape[-1]
    pieces = []
    for p in range(w_ref.shape[0]):
        low, high = max(start, p * size), min(stop, (p + 1) * size)
        if low < high:
            value = w_ref[p, :, :, low - p * size : high - p * size]
            pieces.append((value.reshape(-1, high - low), low - start))
    return pieces


def times_columns(left, w_ref, start, stop):
    return jnp.concatenate([nn(left, value) for value, _ in columns_of(w_ref, start, stop)], axis=1)


def times_transposed(left, w_ref, start, stop):
    out = None
    for value, low in columns_of(w_ref, start, stop):
        term = nt(left[:, low : low + value.shape[1]], value)
        out = term if out is None else out + term
    return out


def prepare_kernel(where, lengths, table, position_ref, band_ref, segq_ref, segk_ref, perm_ref):
    s = where[1]
    shape = segq_ref.shape
    token = lax.broadcasted_iota(jnp.int32, shape, 0)
    lane = lax.broadcasted_iota(jnp.int32, shape, 1)
    segment = jnp.zeros(shape, jnp.int32)
    end = 0
    for j in range(lengths.shape[1]):
        end = end + lengths[s, j]
        segment = segment + (token >= end).astype(jnp.int32)
    same = lane == segment
    segq_ref[...] = jnp.where(same, 1.0, 0.0).astype(BF16)
    segk_ref[...] = jnp.where(same | (lane >= lengths.shape[1]), 0.0, -1e30).astype(BF16)
    offset = lax.broadcasted_iota(jnp.int32, (8, 3 * TILE), 1) - TILE
    bucket = bucket_of(offset)
    near = (TILE, 3 * TILE)
    outside = lax.broadcasted_iota(jnp.int32, near, 1) < lax.broadcasted_iota(jnp.int32, near, 0)
    for h in range(band_ref.shape[0]):
        base = jnp.zeros((8, 3 * TILE), F32)
        for i in range(BUCKETS):
            base = jnp.where(bucket == i, table[i, h], base)
        rows = pltpu.roll(jnp.broadcast_to(base[:1], near), 0, 1, stride=1, stride_axis=0)
        band_ref[h] = jnp.where(outside, table[15, h], rows)
    position = lax.broadcasted_iota(jnp.int32, perm_ref.shape, 0)
    perm_ref[...] = jnp.where(position == position_ref[...], 1.0, 0.0).astype(BF16)


def qkv_kernel(pattern, shard, where, keep_ref, mate_ref, away_ref, far_ref, perm_ref, *refs):
    count = len(pattern) if pattern else 1
    qkv_ref, first_t_ref, x_ref, glow_ref, gains_ref = refs[count : count + 5]
    w_ref = refs[count + 5] if pattern else refs[0]
    if pattern:
        fill(where, [(ref, *entry) for ref, entry in zip(refs, pattern)], w_ref, False)
    size = keep_ref.shape[1]
    width = keep_ref.shape[2]
    for rel in range(4):
        block = where[1] ^ rel
        source = (keep_ref, mate_ref, away_ref.at[0], far_ref)[rel]
        x_ref[block] = source[0]
        glow_ref[block] = source[1]
    gains = gains_of(w_ref, width, shard)
    gains_ref[...] = gains
    x = x_ref[...].reshape(4 * size, width).astype(F32)
    r1 = lax.rsqrt(jnp.mean(x * x, axis=-1, keepdims=True) + EPS)
    first = (x * r1 * gains[:1]).astype(BF16)
    for value, low in columns_of(w_ref, 0, 3 * width):
        qkv_ref[:, low : low + value.shape[1]] = nn(first, value).astype(BF16)
    first_t_ref[...] = nt(perm_ref[...], first).astype(BF16)


def gains_of(w_ref, width, shard):
    size = w_ref.shape[-1]
    spare = w_ref[4 * width // size, :, :, 4 * width % size : 4 * width % size + TILE].astype(F32)
    rows = width // TILE
    if spare.shape[0] > 1:
        together = jnp.sum(spare, axis=0)
        found = [together[k : k + 1] for k in range(2 * rows)]
    else:
        spare = spare.reshape(-1, TILE)
        row = lax.broadcasted_iota(jnp.int32, spare.shape, 0) % shard
        found = [jnp.sum(jnp.where(row == k, spare, 0.0), axis=0, keepdims=True) for k in range(2 * rows)]
    return jnp.concatenate([jnp.concatenate(found[:rows], axis=1), jnp.concatenate(found[rows:], axis=1)], axis=0)


CHUNK = 32


def attention_kernel(first_pair, q_ref, k_ref, v_ref, band_ref, table_ref, segq_ref, segk_ref, probs_ref, ctx_ref, s_ref):
    pair = pl.program_id(0) + first_pair
    length = q_ref.shape[0]
    tiles = length // TILE
    q, v = q_ref[...], v_ref[...]
    lane = lax.broadcasted_iota(jnp.int32, q.shape, 1)
    keys = jnp.concatenate([k_ref[...], segk_ref[...]], axis=1)
    halves = []
    for h in range(2):
        mine = (lane < HEAD_DIM) if h == 0 else (lane >= HEAD_DIM)
        queries = jnp.concatenate([jnp.where(mine, q, jnp.zeros_like(q)), segq_ref[...]], axis=1)
        s_ref[h] = nt(queries, keys)
    for h in range(2):
        below = table_ref[15, 2 * pair + h]
        above = table_ref[31, 2 * pair + h]
        for r in range(0, length, CHUNK):
            t = r // TILE
            parts = []
            for u in range(tiles):
                d = u - t
                part = s_ref[h, r : r + CHUNK, u * TILE : (u + 1) * TILE]
                if abs(d) <= 1:
                    part = part + band_ref[h, r - t * TILE : r - t * TILE + CHUNK, (d + 1) * TILE : (d + 2) * TILE]
                else:
                    part = part + (above if d > 0 else below)
                parts.append(part)
            s = jnp.concatenate(parts, axis=1)
            p = jnp.exp(s - jnp.max(s, axis=-1, keepdims=True))
            p = p * (1.0 / jnp.sum(p, axis=-1, keepdims=True))
            probs_ref[h, r : r + CHUNK, :] = p.astype(BF16)
        halves.append(nn(probs_ref[h], v))
    ctx_ref[...] = jnp.where(lane < HEAD_DIM, halves[0], halves[1]).astype(BF16)


def out_kernel(x_ref, ctx_a_ref, ctx_b_ref, w_ref, gains_ref, perm_ref, attn_ref, second_ref, second_t_ref):
    width = x_ref.shape[1]
    ctx = jnp.concatenate([ctx_a_ref[...], ctx_b_ref[...]], axis=1)
    attn = times_columns(ctx, w_ref, 3 * width, 4 * width)
    attn_ref[...] = attn
    middle = x_ref[...].astype(F32) + attn
    r2 = lax.rsqrt(jnp.mean(middle * middle, axis=-1, keepdims=True) + EPS)
    second = (middle * r2 * gains_ref[1:]).astype(BF16)
    second_ref[...] = second
    second_t_ref[...] = nt(perm_ref[...], second).astype(BF16)


def up_kernel(pattern, place, where, second_ref, glow_ref, *refs):
    if pattern:
        w_ref = refs[-1]

        @pl.when(pl.program_id(0) == 0)
        def _():
            fill(where, [(ref, *entry) for ref, entry in zip(refs, pattern)], w_ref, False)

        weight = w_ref[pl.program_id(0)]
        act_ref, slope_ref, keep_ref, send_ref = refs[len(pattern) : len(pattern) + 4]
        weight = weight.reshape(-1, weight.shape[-1])
    else:
        weight = flat(refs[0])
        act_ref, slope_ref, keep_ref, send_ref = refs[1:]
    up = nn(second_ref[...], weight)
    phi_cap = 0.5 * (1.0 + lax.erf(up * 0.7071067811865476))
    act = (up * phi_cap).astype(BF16)
    act_ref[...] = act
    slope = phi_cap + up * (jnp.exp(-0.5 * up * up) * 0.3989422804014327)
    slope_ref[...] = slope.astype(BF16)
    dwd = tn(act, glow_ref[...])
    if len(keep_ref.shape) == 2:
        keep_ref[...] = dwd.astype(BF16)
    else:
        rows = keep_ref.shape[-2]
        blocks = [dwd[i * rows : (i + 1) * rows].astype(BF16) for i in range(8)]
        for axis, bit in ((1, 4), (2, 2), (3, 1)):
            flip = place[axis] == 1
            blocks = [jnp.where(flip, blocks[i ^ bit], blocks[i]) for i in range(8)]
        core = place[3]
        for ref, c_rel in ((keep_ref, 0), (send_ref, 1)):
            x_outer = core == c_rel
            for i in range(2):
                for j in range(2):
                    one, other = blocks[4 * i + 2 * j + c_rel], blocks[4 * j + 2 * i + c_rel]
                    ref[i, j, 0, 0] = one if i == j else jnp.where(x_outer, one, other)


def down_kernel(pattern, where, second_t_ref, glow_ref, attn_ref, act_ref, slope_ref, win_ref, *refs):
    j = pl.program_id(0)
    win = flat(win_ref)
    count = len(pattern) if pattern else 1
    keep_ref, mate_ref, away_ref, dsec_ref, win_keep_ref, win_send_ref, acc_ref, dacc_ref, hold_ref = refs[count : count + 9]
    if pattern:
        w_ref = refs[-1]

        @pl.when(j == 0)
        def _():
            fill(where, [(ref, *entry) for ref, entry in zip(refs, pattern)], w_ref, True)

        shards = w_ref.shape[0] // 4
        wd = w_ref[pl.ds(j * shards, shards)]
        wd = wd.reshape(-1, wd.shape[-1])
    else:
        wd = flat(refs[0])
    gup = (nt(glow_ref[...], wd) * slope_ref[...].astype(F32)).astype(BF16)
    out = nn(act_ref[...], wd)
    dsec = nt(gup, win)

    @pl.when(j == 0)
    def _():
        acc_ref[...] = attn_ref[...] + out
        dacc_ref[...] = dsec

    @pl.when(j > 0)
    def _():
        acc_ref[...] += out
        dacc_ref[...] += dsec

    @pl.when(j == pl.num_programs(0) - 1)
    def _():
        place_rows(where, acc_ref[...], keep_ref, mate_ref, away_ref, hold_ref)
        dsec_ref[...] = dacc_ref[...]

    dwin = nn(second_t_ref[...], gup).astype(BF16)
    half = dwin.shape[0] // 2
    win_keep_ref[...] = dwin[:half]
    win_send_ref[...] = dwin[half:]


def mid_kernel(
    x_ref, attn_ref, gains_ref, dsec_ref, glow_ref, ctx_a_ref, ctx_b_ref, perm_ref, w_ref,
    gmd_ref, g2_ref, dctx_ref, keep_ref, send_ref,
):
    middle = x_ref[...].astype(F32) + attn_ref[...]
    r2 = lax.rsqrt(jnp.mean(middle * middle, axis=-1, keepdims=True) + EPS)
    normed = middle * r2
    dsec = dsec_ref[...]
    g2_ref[...] = jnp.sum(dsec * normed, axis=0, keepdims=True)
    scaled = dsec * gains_ref[1:]
    gmd = r2 * (scaled - normed * jnp.mean(scaled * normed, axis=-1, keepdims=True))
    gmd_ref[...] = gmd
    low = (glow_ref[...].astype(F32) + gmd).astype(BF16)
    dctx_ref[...] = times_transposed(low, w_ref, 3 * low.shape[1], 4 * low.shape[1]).astype(BF16)
    ctx_t = nt(perm_ref[...], jnp.concatenate([ctx_a_ref[...], ctx_b_ref[...]], axis=1)).astype(BF16)
    dw = nn(ctx_t, low).astype(BF16)
    half = dw.shape[0] // 2
    keep_ref[...] = dw[:half]
    send_ref[...] = dw[half:]


def back_kernel(q_ref, k_ref, v_ref, dctx_ref, ctx_ref, probs_ref, dq_ref, dk_ref, dv_ref, sums_ref, ds_ref, dp_ref, near_ref):
    length = q_ref.shape[0]
    tiles = length // TILE
    q, k, v, dctx = q_ref[...], k_ref[...], v_ref[...], dctx_ref[...]
    lane = lax.broadcasted_iota(jnp.int32, (length, TILE), 1)
    product = dctx.astype(F32) * ctx_ref[...].astype(F32)
    square = lambda axis: lax.broadcasted_iota(jnp.int32, (TILE, TILE), axis)
    turn = (square(0) + square(1) == TILE - 1).astype(F32)
    row = lax.broadcasted_iota(jnp.int32, (TILE, 3 * TILE), 0)
    column = lax.broadcasted_iota(jnp.int32, (TILE, 3 * TILE), 1)
    dqs, dk, dv = [], None, None

    def put(old, new):
        return new if old is None else old + new

    masked = []
    for h in range(2):
        mine = (lane < HEAD_DIM) if h == 0 else (lane >= HEAD_DIM)
        do = jnp.where(mine, dctx, jnp.zeros_like(dctx))
        dp_ref[h] = nt(do, v)
        masked.append((mine, do))
    for h in range(2):
        mine, do = masked[h]
        delta = jnp.sum(jnp.where(mine, product, 0.0), axis=-1, keepdims=True)
        far = [None, None]
        for start in range(0, TILE, CHUNK):
            band = [None, None, None]
            for t in range(tiles):
                rows = slice(t * TILE + start, t * TILE + start + CHUNK)
                ds = probs_ref[h, rows, :].astype(F32) * (dp_ref[h, rows, :] - delta[rows])
                ds_ref[h, rows, :] = ds.astype(BF16)
                for u in range(tiles):
                    d = u - t
                    part = ds[:, u * TILE : (u + 1) * TILE]
                    if abs(d) <= 1:
                        band[d + 1] = put(band[d + 1], part)
                    else:
                        far[int(d > 0)] = put(far[int(d > 0)], part)
            near_ref[start : start + CHUNK, :] = jnp.concatenate(band, axis=1)
        near = near_ref[...]
        outside = jnp.where(column < row, near, 0.0)
        near = jnp.where(column < row, 0.0, near)
        near = lax.dot_general(turn, near, (((1,), (0,)), ((), ())), precision=HIGHEST, preferred_element_type=F32)
        near = pltpu.roll(near, 0, 1, stride=1, stride_axis=0)
        sums_ref[0, h : h + 1, :] = jnp.sum(near, axis=0, keepdims=True)
        sums_ref[0, 2 + h : 3 + h, :] = jnp.sum(outside, axis=0, keepdims=True)
        for i in range(2):
            sums_ref[0, 4 + 2 * i + h : 5 + 2 * i + h, :TILE] = jnp.sum(far[i], axis=0, keepdims=True)
            sums_ref[0, 4 + 2 * i + h : 5 + 2 * i + h, TILE:] = jnp.zeros((1, 2 * TILE), F32)
        dqs.append(nn(ds_ref[h], k))
        dk = put(dk, tn(ds_ref[h], jnp.where(mine, q, jnp.zeros_like(q))))
        dv = put(dv, tn(probs_ref[h], do))
    dq_ref[...] = jnp.where(lane < HEAD_DIM, dqs[0], dqs[1]).astype(BF16)
    dk_ref[...] = dk.astype(BF16)
    dv_ref[...] = dv.astype(BF16)


def grad_kernel(dqa_ref, dqb_ref, dka_ref, dkb_ref, dva_ref, dvb_ref, first_t_ref, keep_ref, send_ref):
    refs = (dqa_ref, dqb_ref, dka_ref, dkb_ref, dva_ref, dvb_ref)
    dw = nn(first_t_ref[...], jnp.concatenate([ref[...] for ref in refs], axis=1)).astype(BF16)
    half = dw.shape[0] // 2
    keep_ref[...] = dw[:half]
    send_ref[...] = dw[half:]


def first_kernel(
    where, x_ref, gains_ref, dqa_ref, dqb_ref, dka_ref, dkb_ref, dva_ref, dvb_ref, w_ref, gmd_ref,
    row_keep_ref, row_mate_ref, row_away_ref, g1_ref, hold_ref,
):
    width = x_ref.shape[1]
    x = x_ref[...].astype(F32)
    r1 = lax.rsqrt(jnp.mean(x * x, axis=-1, keepdims=True) + EPS)
    normed = x * r1
    refs = (dqa_ref, dqb_ref, dka_ref, dkb_ref, dva_ref, dvb_ref)
    dfirst = times_transposed(jnp.concatenate([ref[...] for ref in refs], axis=1), w_ref, 0, 3 * width)
    g1_ref[...] = jnp.sum(dfirst * normed, axis=0, keepdims=True)
    scaled = dfirst * gains_ref[:1]
    delta = gmd_ref[...] + r1 * (scaled - normed * jnp.mean(scaled * normed, axis=-1, keepdims=True))
    place_rows(where, delta, row_keep_ref, row_mate_ref, row_away_ref, hold_ref)


def shape(dims, dtype):
    return jax.ShapeDtypeStruct(tuple(dims), dtype)


def after(value, *earlier):
    return lax.optimization_barrier((value,) + earlier)[0]


def total(*parts):
    sums = parts[0].astype(F32)
    for part in parts[1:]:
        sums = sums + part.astype(F32)
    return sums


def on_device(
    nb, ns, hidden_in, doc_lengths, bias_table, gain_attn, gain_ffn,
    w_query, w_key, w_value, w_out, w_in, w_down, out_grad,
):
    rows_dev, shard_len, width = hidden_in.shape
    length = ns * shard_len
    ff = w_in.shape[1]
    shard = w_query.shape[0]
    b, s = lax.axis_index("batch"), lax.axis_index("seq")
    y, c = s // 2, s % 2
    bits = [1 << i for i in range(1, nb.bit_length() - 1)]
    gather_order = ([1] + bits[::-1], bits[::-1] + [1])

    def masks(core):
        value = [0]
        for bit in gather_order[core]:
            value = value + [old ^ bit for old in value]
        return value

    where = jnp.concatenate([jnp.stack([b, s]), jnp.array(masks(0) + masks(1))]).astype(jnp.int32)

    def move(value, first, second=None):
        pairs = []
        for i in range(nb):
            for j in range(ns):
                bm, sm = second if second is not None and j % 2 else first
                pairs.append((i * ns + j, (i ^ bm) * ns + (j ^ sm)))
        return lax.ppermute(value, ("batch", "seq"), pairs)

    core = lambda value: move(value, (0, 1))
    other_y = lambda value: move(value, (0, 2))

    def piece(weight, parts, axis=1):
        size = weight.shape[axis] // parts
        return lax.dynamic_slice_in_dim(weight, (c if parts == 2 else s) * size, size, axis)[None]

    def step(block, i):
        return move(block, (gather_order[0][i], 0), (gather_order[1][i], 0))

    tiled = (shard // 2) % 16 == 0

    def plain(pieces, rows_last=False):
        parts = 4 if any(entry[1] > 1 for entry in pieces) else 2
        dims = pieces[0][0].shape[1:]
        full = jnp.zeros((parts, nb) + dims, BF16)
        for array, flip, base in pieces:
            part = s ^ flip if parts == 4 else (s ^ flip) % 2
            shards = b ^ jnp.where((s ^ flip) % 2 == 0, jnp.array(masks(0)), jnp.array(masks(1)))
            full = full.at[part, shards[base : base + array.shape[0]]].set(array)
        if rows_last:
            return jnp.swapaxes(full, 0, 1)
        return full.reshape(parts, 1, nb * dims[0], dims[1])

    def assemble(name, pieces, rows_last=False):
        if not tiled:
            return plain(pieces, rows_last)
        arrays = [entry[0] for entry in pieces]
        parts = 4 if any(entry[1] > 1 for entry in pieces) else 2
        return pl.pallas_call(
            functools.partial(weight_kernel, [entry[1:] for entry in pieces], rows_last),
            name=name,
            out_shape=shape(((nb, parts) if rows_last else (parts, nb)) + arrays[0].shape[1:], BF16),
            in_specs=[smem] + [vmem] * len(arrays),
            cost_estimate=cost(5),
            compiler_params=params(),
        )(where, *arrays)

    vmem = pl.BlockSpec(memory_space=pltpu.VMEM)
    smem = pl.BlockSpec(memory_space=pltpu.SMEM)
    stages = len(bits) + 1

    def grow(block, start, stop, *gates):
        for i in range(start, stop):
            block = jnp.concatenate([block, after(step(block, i), *gates)])
        return block

    per = width // (nb * ns)
    feature = jnp.arange(width)
    fb, fs, fr = feature // (per * ns), feature // per % ns, feature % per
    b_rel, s_rel = fb ^ b, fs ^ s
    x_rel, y_rel = b_rel % 2, s_rel // 2
    swapped = fs % 2 == 1
    position = (s_rel % 2) * 2 + jnp.where(swapped, y_rel, x_rel)
    position = position * 2 + jnp.where(swapped, x_rel, y_rel)
    for bit in bits:
        position = position * 2 + (b_rel & bit) // bit
    position = (position * per + fr).reshape(1, width)

    own = jnp.zeros((2, width), BF16)
    own = lax.dynamic_update_slice(own, jnp.stack([gain_attn, gain_ffn]), (0, b * shard)).reshape(-1, TILE)
    own = jnp.pad(own, ((0, shard - own.shape[0]), (0, TILE)))
    block1 = piece(jnp.concatenate([w_query, w_key, w_value, w_out, own], axis=1), 2)
    row_keep, row_mate, row_away = pl.pallas_call(
        pack_kernel,
        name="pack",
        out_shape=(
            shape((2, shard_len, width), BF16), shape((2, shard_len, width), BF16), shape((2, 2, shard_len, width), BF16),
        ),
        in_specs=[smem, vmem, vmem],
        cost_estimate=cost(3),
        compiler_params=params(),
    )(where, hidden_in, out_grad)
    row_got = other_y(row_away)
    band, seg_queries, seg_keys, perm = pl.pallas_call(
        prepare_kernel,
        name="prepare",
        out_shape=(
            shape((HEADS, TILE, 3 * TILE), F32), shape((length, TILE), BF16), shape((length, TILE), BF16),
            shape((width, width), BF16),
        ),
        in_specs=[smem, smem, smem, vmem],
        cost_estimate=cost(6),
        compiler_params=params(),
    )(where, doc_lengths, bias_table, position)
    start1 = grow(block1, 0, 1)
    low1 = grow(start1, 1, stages - 1, row_got, band)
    high1 = step(low1, stages - 1)
    row_mate, row_far = core(row_mate), core(row_got[1])
    low2 = grow(piece(after(w_in, start1), 4), 0, stages - 1)
    high1 = after(high1, low2)
    gather1 = [(low1, 0, 0), (high1, 0, nb // 2), (core(low1), 1, 0), (core(high1), 1, nb // 2)]
    high2 = step(low2, stages - 1)
    y_low2 = other_y(low2)
    block3 = piece(after(w_down, low2), 4, 0)
    gather1[0] = (after(low1, block3), 0, 0)
    row_block = shape((4, shard_len, width), BF16)
    w1_shape = shape((2, nb) + low1.shape[1:], BF16)
    pieces1 = [entry[0] for entry in gather1] if tiled else [plain(gather1)]
    outputs = pl.pallas_call(
        functools.partial(qkv_kernel, [entry[1:] for entry in gather1] if tiled else None, shard),
        name="qkv",
        out_shape=(
            shape((length, 3 * width), BF16), shape((width, length), BF16), row_block, row_block, shape((2, width), F32),
            *([w1_shape] if tiled else []),
        ),
        in_specs=[smem] + [vmem] * (5 + len(pieces1)),
        cost_estimate=cost(9),
        compiler_params=params(),
    )(where, row_keep, row_mate, row_got, row_far, perm, *pieces1)
    qkv, first_t, xb, glow, gains = outputs[:5]
    w1 = outputs[5] if tiled else pieces1[0]
    xb, glow = xb.reshape(length, width), glow.reshape(length, width)

    y_high2 = other_y(after(high2, qkv))
    mid3 = grow(block3, 0, stages - 2, qkv)

    pairs = HEADS // 4
    pair_block = lambda first: pl.BlockSpec((length, TILE), lambda p: (0, first + p))
    head_block = lambda first, *dims: pl.BlockSpec((2,) + dims, lambda p: (first + p,) + (0,) * len(dims))
    whole_block = lambda *dims: pl.BlockSpec(dims, lambda p: (0,) * len(dims))

    def attend(i, gated):
        return pl.pallas_call(
            functools.partial(attention_kernel, i * pairs),
            name="attention",
            grid=(pairs,),
            out_shape=(shape((HEADS // 2, length, length), BF16), shape((length, width // 2), BF16)),
            in_specs=[
                pair_block(i * pairs), pair_block((2 + i) * pairs), pair_block((4 + i) * pairs),
                head_block(i * pairs, TILE, 3 * TILE), smem, whole_block(length, TILE), whole_block(length, TILE),
            ],
            out_specs=(head_block(0, length, length), pair_block(0)),
            scratch_shapes=[pltpu.VMEM((2, length, length), F32)],
            cost_estimate=cost(10),
            compiler_params=params(),
        )(qkv, qkv, qkv, gated, bias_table, seg_queries, seg_keys)

    probs_a, ctx_a = attend(0, after(band, high2, mid3, y_low2))
    low3 = grow(mid3, stages - 2, stages - 1, ctx_a)
    probs_b, ctx_b = attend(1, after(band, low3, y_high2))
    high3 = after(step(low3, stages - 1), ctx_b)
    y_low3 = other_y(after(low3, y_high2))
    y_high3 = other_y(high3)
    gather3 = [
        (low3, 0, 0), (high3, 0, nb // 2), (core(low3), 1, 0), (core(high3), 1, nb // 2),
        (y_low3, 2, 0), (y_high3, 2, nb // 2), (core(y_low3), 3, 0), (core(y_high3), 3, nb // 2),
    ]

    gather2 = [
        (low2, 0, 0), (high2, 0, nb // 2), (core(low2), 1, 0), (core(high2), 1, nb // 2),
        (y_low2, 2, 0), (y_high2, 2, nb // 2),
        (core(after(y_low2, qkv)), 3, 0), (core(after(y_high2, ctx_a)), 3, nb // 2),
    ]
    attn, second, second_t = pl.pallas_call(
        out_kernel,
        name="out",
        out_shape=(shape((length, width), F32), shape((length, width), BF16), shape((width, length), BF16)),
        cost_estimate=cost(5),
        compiler_params=params(),
    )(xb, after(ctx_a, high3), ctx_b, w1, gains, perm)

    steps = 4
    part = ff // steps
    per_down = ff // (nb * ns)
    aligned = nb == 2 * steps and per_down % 16 == 0
    if aligned:

        def wd_index(j, place):
            rel = j ^ place[0]
            return 0, 0, rel % 2, rel // 2, 0, 0

        wd_block = pl.BlockSpec((2, 2, 1, 1, per_down, width), wd_index)
        wd_shape = shape((2, 2, 2, 2, per_down, width), BF16)
        wd_shapes, wd_blocks = (wd_shape, wd_shape), (wd_block, wd_block)
    else:
        wd_shapes = (shape((ff, width), BF16), shape((8, TILE), BF16))
        wd_blocks = (
            pl.BlockSpec((part, width), lambda j, place: (j, 0)),
            pl.BlockSpec((8, TILE), lambda j, place: (0, 0)),
        )
    place = jnp.stack([b // 2, b % 2, y, c]).astype(jnp.int32)
    full = lambda *dims: pl.BlockSpec(dims, lambda j, *place: (0,) * len(dims))
    half = width // 2
    column_block = lambda r: pl.BlockSpec((r, part), lambda j, *place: (0, j))
    win_shape = (4, nb) + low2.shape[1:]
    pieces2 = [entry[0] for entry in gather2] if tiled else [plain(gather2)]
    win_shape = win_shape if tiled else pieces2[0].shape
    win_block = pl.BlockSpec((1,) + win_shape[1:], lambda j, *place: (j, 0, 0, 0))
    always = lambda array: pl.BlockSpec(array.shape, lambda j, *place: (0,) * array.ndim)
    outputs = pl.pallas_call(
        functools.partial(up_kernel, [entry[1:] for entry in gather2] if tiled else None),
        name="up",
        out_shape=(
            shape((length, ff), BF16), shape((length, ff), BF16), *wd_shapes, *([shape(win_shape, BF16)] if tiled else []),
        ),
        grid_spec=pltpu.PrefetchScalarGridSpec(
            num_scalar_prefetch=1,
            grid=(steps,),
            in_specs=[smem, full(length, width), full(length, width)]
            + ([always(array) for array in pieces2] if tiled else [win_block]),
            out_specs=(
                column_block(length), column_block(length), *wd_blocks, *([full(*win_shape)] if tiled else []),
            ),
        ),
        cost_estimate=cost(10),
        compiler_params=params(),
    )(place, where, after(second, y_low3, y_high3), glow, *pieces2)
    act, slope, wd_keep, wd_send = outputs[:4]
    win = outputs[4] if tiled else pieces2[0]

    scatter_masks = [((1, 0), (0, 2)), ((0, 2), (1, 0))] + [((bit, 0), (bit, 0)) for bit in bits]

    class Scatter:
        def __init__(self, *held):
            self.held = list(held)
            self.rows = held[0].shape[0]
            self.i = 0

        def outgoing(self):
            self.sent = total(*[value[self.rows // 2 : self.rows] for value in self.held]).astype(BF16)
            return self.sent

        def send(self):
            self.got = move(self.sent, *scatter_masks[self.i])

        def take(self, *gates):
            self.i += 1
            self.rows //= 2
            self.held.append(after(self.got, *gates))

        def result(self):
            return total(*[value[: self.rows] for value in self.held])

    if not aligned:
        blocks = wd_keep.reshape(nb, ns, per_down, width)

        def order(dest):
            index = jnp.arange(nb * 2)
            digits = [(index >> (stages - i)) % 2 for i in range(stages + 1)]
            x_bit = jnp.where(dest == 0, digits[0], digits[1])
            y_bit = jnp.where(dest == 0, digits[1], digits[0])
            shards = x_bit
            for bit, digit in zip(bits, digits[2:]):
                shards = shards + bit * digit
            return blocks[shards ^ b, 2 * (y_bit ^ y) + dest]

        wd_keep, wd_send = order(c), order(1 - c)
    wd_keep, wd_send = wd_keep.reshape(ff // 2, width), wd_send.reshape(ff // 2, width)
    down = Scatter(wd_keep, core(wd_send))
    down_sent = down.outgoing()
    down.send()

    pieces3 = [entry[0] for entry in gather3] if tiled else [plain(gather3, True)]
    wd_dims = (nb, 4) + low3.shape[1:]
    wd_spec = pl.BlockSpec((nb // steps,) + wd_dims[1:], lambda j: (j, 0, 0, 0))
    row_shapes = (shape((shard_len, width), BF16),) * 2 + (shape((2, shard_len, width), BF16),)
    row_specs = (full(shard_len, width), full(shard_len, width), full(2, shard_len, width))
    hold = pltpu.VMEM((4, shard_len, width), BF16)
    out_keep, out_mate, out_away, dsec, win_keep, win_send = pl.pallas_call(
        functools.partial(down_kernel, [entry[1:] for entry in gather3] if tiled else None),
        name="down",
        grid=(steps,),
        out_shape=(*row_shapes, shape((length, width), F32), shape((half, ff), BF16), shape((half, ff), BF16)),
        in_specs=[
            smem, full(width, length), full(length, width), full(length, width), column_block(length),
            column_block(length), win_block, *([always(array) for array in pieces3] if tiled else [wd_spec]),
        ],
        out_specs=(*row_specs, full(length, width), column_block(half), column_block(half)),
        scratch_shapes=[
            pltpu.VMEM((length, width), F32), pltpu.VMEM((length, width), F32), hold,
            *([pltpu.VMEM(wd_dims, BF16)] if tiled else []),
        ],
        cost_estimate=cost(15),
        compiler_params=params(),
    )(where, second_t, glow, attn, after(act, down_sent), slope, win, *pieces3)
    win_got = core(win_send)
    out_got = other_y(out_away)

    gmd, g2, dctx, wo_keep, wo_send = pl.pallas_call(
        mid_kernel,
        name="mid",
        out_shape=(
            shape((length, width), F32), shape((1, width), F32), shape((length, width), BF16),
            shape((half, width), BF16), shape((half, width), BF16),
        ),
        cost_estimate=cost(7),
        compiler_params=params(),
    )(xb, attn, gains, dsec, glow, ctx_a, ctx_b, perm, w1)
    wo_got = core(wo_send)
    both = Scatter(
        jnp.concatenate([win_keep, wo_keep], axis=1), jnp.concatenate([after(win_got, dctx), wo_got], axis=1)
    )
    both_sent = both.outgoing()
    both.send()
    down.take(both_sent)
    down_sent = down.outgoing()
    down.send()

    def back(i, gated):
        return pl.pallas_call(
            back_kernel,
            name="back",
            grid=(pairs,),
            out_shape=(*(shape((length, width // 2), BF16),) * 3, shape((pairs, 8, 3 * TILE), F32)),
            in_specs=[
                pair_block(i * pairs), pair_block((2 + i) * pairs), pair_block((4 + i) * pairs),
                pair_block(i * pairs), pair_block(0), head_block(0, length, length),
            ],
            out_specs=(*(pair_block(0),) * 3, pl.BlockSpec((1, 8, 3 * TILE), lambda p: (p, 0, 0))),
            scratch_shapes=[
                pltpu.VMEM((2, length, length), BF16), pltpu.VMEM((2, length, length), F32), pltpu.VMEM((TILE, 3 * TILE), F32),
            ],
            cost_estimate=cost(10),
            compiler_params=params(),
        )(qkv, qkv, qkv, gated, (ctx_a, ctx_b)[i], (probs_a, probs_b)[i])

    dq_a, dk_a, dv_a, sums_a = back(0, after(dctx, down_sent, both_sent))
    down.take(dq_a)
    down_sent = down.outgoing()
    down.send()
    dq_b, dk_b, dv_b, sums_b = back(1, after(dctx, down_sent))
    both.take(dq_b)
    both_sent = both.outgoing()
    both.send()
    down.take(dq_b)
    down_sent = down.outgoing()
    down.send()

    grads = (after(dq_a, down_sent, both_sent), dq_b, dk_a, dk_b, dv_a, dv_b)
    keep, send = pl.pallas_call(
        grad_kernel,
        name="grad",
        out_shape=(shape((half, 3 * width), BF16),) * 2,
        cost_estimate=cost(5),
        compiler_params=params(),
    )(*grads, first_t)
    last_got = core(send)
    both.take(send)
    both_sent = both.outgoing()
    both.send()
    in_keep, in_mate, in_away, g1 = pl.pallas_call(
        first_kernel,
        name="first",
        out_shape=(*row_shapes, shape((1, width), F32)),
        in_specs=[smem] + [vmem] * 10,
        scratch_shapes=[hold],
        cost_estimate=cost(6),
        compiler_params=params(),
    )(where, xb, gains, after(grads[0], send, both_sent), *grads[1:], w1, gmd)
    last = Scatter(keep, after(last_got, g1))
    last_sent = last.outgoing()
    last.send()
    both.take(last_sent)
    while both.i < stages + 1:
        both.outgoing()
        both.send()
        both.take()
    op1_sent = last_sent
    in_got = other_y(after(in_away, last_sent))

    sums = jnp.concatenate([sums_a, after(sums_b, last_sent)])
    near = sums[:, :2].reshape(HEADS, 3 * TILE)
    outer = jnp.sum(sums[:, 2:], axis=-1).reshape(HEADS // 2, 3, 2)
    below, above = (outer[:, 0] + outer[:, 1]).reshape(HEADS), outer[:, 2].reshape(HEADS)
    offset_bucket = bucket_of((jnp.arange(3 * TILE) - (TILE - 1)) % (3 * TILE) - TILE)
    bucket_column = jnp.arange(BUCKETS)[:, None]
    table = jnp.dot((bucket_column == offset_bucket[None, :]).astype(F32), near.T, precision=HIGHEST)
    table = table + jnp.where(bucket_column == 15, below, 0.0) + jnp.where(bucket_column == 31, above, 0.0)
    table = jnp.pad(table.reshape(-1, TILE), ((0, 1), (0, 0)))
    small = jnp.concatenate([g1.reshape(-1, TILE), g2.reshape(-1, TILE), table])
    small_masks = [(0, 1), (0, 2), (1, 0)] + [(bit, 0) for bit in bits]

    small = small + move(after(small, last_sent), small_masks[0])
    last.take()
    last_sent = last.outgoing()
    small = small + move(after(small, last_sent), small_masks[1])
    last.send()
    for i in range(2, stages + 1):
        last.take()
        last_sent = last.outgoing()
        last.send()
        small = small + move(after(small, last_sent), small_masks[i])
    small = small + move(small, small_masks[stages + 1])
    last.take()
    down.take(last_sent)
    while down.i < stages + 1:
        down.outgoing()
        down.send()
        down.take()
    down_grad_w = down.result()
    both_sum, last_sum = both.result(), last.result()
    gain_rows_count = width // TILE
    gain_grads = small[: 2 * gain_rows_count].reshape(2, width)
    gain_grads = lax.dynamic_slice_in_dim(gain_grads, (b * ns + s) * per, per, 1)
    table = small[2 * gain_rows_count : 2 * gain_rows_count + BUCKETS * HEADS // TILE].reshape(BUCKETS, HEADS)

    def unpack(name, old, keep, mate, got):
        mate, far = core(after(mate, got)), core(got[1])
        return pl.pallas_call(
            unpack_kernel,
            name=name,
            out_shape=shape(old.shape, F32),
            in_specs=[smem] + [vmem] * 5,
            cost_estimate=cost(3),
            compiler_params=params(),
        )(where, old, keep, mate, got, far)

    out_hidden = unpack("out_rows", hidden_in, out_keep, out_mate, after(out_got, op1_sent))
    input_grad = unpack("in_rows", out_grad, in_keep, in_mate, in_got)
    return (
        out_hidden,
        input_grad,
        table,
        gain_grads[0],
        gain_grads[1],
        last_sum[:, :width],
        last_sum[:, width : 2 * width],
        last_sum[:, 2 * width :],
        both_sum[:, ff:],
        both_sum[:, :ff],
        down_grad_w,
    )


def solution(mesh):
    nb, ns = mesh.shape["batch"], mesh.shape["seq"]
    placed = (
        P("batch", "seq", None),
        P("batch", None),
        P(),
        P("batch"),
        P("batch"),
        P("batch", None),
        P("batch", None),
        P("batch", None),
        P("batch", None),
        P("batch", None),
        P("batch", None),
        P("batch", "seq", None),
    )
    both = ("batch", "seq")
    return jax.shard_map(
        functools.partial(on_device, nb, ns),
        mesh=mesh,
        in_specs=placed,
        out_specs=(
            P("batch", "seq", None),
            P("batch", "seq", None),
            P(),
            P(both),
            P(both),
            P(both, None),
            P(both, None),
            P(both, None),
            P(both, None),
            P(both, None),
            P(both, None),
        ),
        check_vma=False,
    )
```

```python
import functools

import jax
import jax.numpy as jnp
from jax import lax
from jax.experimental import pallas as pl
from jax.experimental.pallas import tpu as pltpu
from jax.sharding import PartitionSpec as P

HEADS = 12
HEAD_DIM = 64
BUCKETS = 32
TILE = 128

EPS = 1e-06
THRESHOLDS = (12, 16, 23, 32, 46, 64, 91)
HIGHEST = lax.Precision.HIGHEST
F32 = jnp.float32
BF16 = jnp.bfloat16
VMEM_LIMIT = 56 * 1024 * 1024


def bucket_of(offsets):
    distance = jnp.abs(offsets)
    stepped = jnp.full_like(distance, 8)
    for threshold in THRESHOLDS:
        stepped = stepped + (distance >= threshold).astype(jnp.int32)
    closer = jnp.where(distance < 8, distance, stepped)
    return closer + 16 * (offsets > 0).astype(jnp.int32)


def nn(left, right):
    return lax.dot_general(left, right, (((1,), (0,)), ((), ())), preferred_element_type=F32)


def nt(left, right):
    return lax.dot_general(left, right, (((1,), (1,)), ((), ())), preferred_element_type=F32)


def tn(left, right):
    return lax.dot_general(left, right, (((0,), (0,)), ((), ())), preferred_element_type=F32)


def params(**kw):
    return pltpu.CompilerParams(vmem_limit_bytes=VMEM_LIMIT, **kw)


def cost(microseconds):
    return pl.CostEstimate(flops=int(microseconds * 1e9), bytes_accessed=int(microseconds * 3.5e6), transcendentals=0)


def pack_kernel(where, hidden_ref, grad_ref, *refs):
    for source, (keep_ref, mate_ref, away_ref) in ((hidden_ref, refs[:3]), (grad_ref, refs[3:])):
        for rel in range(4):
            target = (keep_ref, mate_ref, away_ref.at[0], away_ref.at[1])[rel]
            target[...] = source[where[1] ^ rel].astype(BF16)


def row_of(where, refs, out):
    for rel in range(4):
        source = (refs[0], refs[1], refs[2].at[0], refs[3])[rel]
        out[where[1] ^ rel] = source[...]


def unpack_kernel(where, old_ref, keep_ref, mate_ref, away_ref, far_ref, new_ref):
    for rel in range(4):
        row = where[1] ^ rel
        source = (keep_ref[...], mate_ref[...], away_ref[0], far_ref[...])[rel]
        new_ref[row] = old_ref[row] + source.astype(F32)


def place_rows(where, value, keep_ref, mate_ref, away_ref, hold_ref):
    size = keep_ref.shape[0]
    hold_ref[...] = value.astype(BF16).reshape(4, size, value.shape[1])
    for rel in range(4):
        target = (keep_ref, mate_ref, away_ref.at[0], away_ref.at[1])[rel]
        target[...] = hold_ref[where[1] ^ rel]


def fill(where, pattern, refs, out, rows_last):
    b, s = where[0], where[1]
    parts, shards = (out.shape[1], out.shape[0]) if rows_last else (out.shape[0], out.shape[1])
    size = out.shape[2] if rows_last else out.shape[3]
    rows = out.shape[2]
    for p in range(parts):
        if rows_last:
            out[b, p] = refs[0][p * size : (p + 1) * size, :]
        else:
            out[p, b] = refs[0][:, p * size : (p + 1) * size]
    for ref, (flip, base) in zip(refs[1:], pattern):
        core = (s ^ flip) % 2
        part = (s ^ flip) if parts == 4 else core
        for i in range(ref.shape[0]):
            t = b ^ where[2 + core * shards + base + i]
            if rows_last:
                out[t, part] = ref[i, :rows, :]
            else:
                out[part, t] = ref[i, :rows, :]


def fill_rows(where, pattern, refs, out, first):
    b, s = where[0], where[1]
    shard = refs[0].shape[0]
    shards = out.shape[0] // shard
    quarter = shard // 4
    out[pl.ds(pl.multiple_of(b * shard, 8), shard), :] = refs[0][...].astype(F32)
    for ref, (flip, base) in zip(refs[1:], pattern):
        for i in range(ref.shape[0]):
            t = b ^ where[2 + (s ^ flip) % 2 * shards + base + i]
            low = pl.multiple_of(t * shard + (s ^ flip) * quarter, 8)
            out[pl.ds(low, quarter), :] = ref[i, first : first + quarter, :].astype(F32)


def flat(ref):
    return ref[...].reshape(-1, ref.shape[-1])


def columns_of(w_ref, start, stop):
    size = w_ref.shape[-1]
    pieces = []
    for p in range(w_ref.shape[0]):
        low, high = max(start, p * size), min(stop, (p + 1) * size)
        if low < high:
            value = w_ref[p, :, :, low - p * size : high - p * size]
            pieces.append((value.reshape(-1, high - low), low - start))
    return pieces


def times_columns(left, w_ref, start, stop):
    return jnp.concatenate([nn(left, value) for value, _ in columns_of(w_ref, start, stop)], axis=1)


def times_transposed(left, w_ref, start, stop):
    out = None
    for value, low in columns_of(w_ref, start, stop):
        term = nt(left[:, low : low + value.shape[1]], value)
        out = term if out is None else out + term
    return out


def prepare_kernel(where, lengths, table, position_ref, band_ref, segq_ref, segk_ref, perm_ref):
    s = where[1]
    shape = segq_ref.shape
    token = lax.broadcasted_iota(jnp.int32, shape, 0)
    lane = lax.broadcasted_iota(jnp.int32, shape, 1)
    segment = jnp.zeros(shape, jnp.int32)
    end = 0
    for j in range(lengths.shape[1]):
        end = end + lengths[s, j]
        segment = segment + (token >= end).astype(jnp.int32)
    same = lane == segment
    segq_ref[...] = jnp.where(same, 1.0, 0.0).astype(BF16)
    segk_ref[...] = jnp.where(same | (lane >= lengths.shape[1]), 0.0, -1e30).astype(BF16)
    offset = lax.broadcasted_iota(jnp.int32, (8, 3 * TILE), 1) - TILE
    bucket = bucket_of(offset)
    near = (TILE, 3 * TILE)
    outside = lax.broadcasted_iota(jnp.int32, near, 1) < lax.broadcasted_iota(jnp.int32, near, 0)
    for h in range(band_ref.shape[0]):
        base = jnp.zeros((8, 3 * TILE), F32)
        for i in range(BUCKETS):
            base = jnp.where(bucket == i, table[i, h], base)
        rows = pltpu.roll(jnp.broadcast_to(base[:1], near), 0, 1, stride=1, stride_axis=0)
        band_ref[h] = jnp.where(outside, table[15, h], rows)
    position = lax.broadcasted_iota(jnp.int32, perm_ref.shape, 0)
    perm_ref[...] = jnp.where(position == position_ref[...], 1.0, 0.0).astype(BF16)


def qkv_kernel(pattern, shard, where, keep_ref, mate_ref, away_ref, far_ref, perm_ref, *refs):
    count = len(pattern) + 1 if pattern else 1
    qkv_ref, first_t_ref, x_ref, gains_ref = refs[count : count + 4]
    w_ref = refs[count + 4] if pattern else refs[0]
    if pattern:
        fill(where, pattern, refs[:count], w_ref, False)
    size, width = keep_ref.shape
    row_of(where, (keep_ref, mate_ref, away_ref, far_ref), x_ref)
    gains = gains_of(w_ref, width, shard)
    gains_ref[...] = gains
    x = x_ref[...].reshape(4 * size, width).astype(F32)
    r1 = lax.rsqrt(jnp.mean(x * x, axis=-1, keepdims=True) + EPS)
    first = (x * r1 * gains[:1]).astype(BF16)
    for value, low in columns_of(w_ref, 0, 3 * width):
        qkv_ref[:, low : low + value.shape[1]] = nn(first, value).astype(BF16)
    first_t_ref[...] = nt(perm_ref[...], first).astype(BF16)


def gains_of(w_ref, width, shard):
    size = w_ref.shape[-1]
    spare = w_ref[3 * width // size, :, :, 3 * width % size : 3 * width % size + TILE].astype(F32)
    rows = width // TILE
    if spare.shape[0] > 1:
        together = jnp.sum(spare, axis=0)
        found = [together[k : k + 1] for k in range(2 * rows)]
    else:
        spare = spare.reshape(-1, TILE)
        row = lax.broadcasted_iota(jnp.int32, spare.shape, 0) % shard
        found = [jnp.sum(jnp.where(row == k, spare, 0.0), axis=0, keepdims=True) for k in range(2 * rows)]
    return jnp.concatenate([jnp.concatenate(found[:rows], axis=1), jnp.concatenate(found[rows:], axis=1)], axis=0)


CHUNK = 32


def attention_kernel(first_pair, q_ref, k_ref, v_ref, band_ref, table_ref, segq_ref, segk_ref, probs_ref, ctx_ref, s_ref):
    pair = pl.program_id(0) + first_pair
    length = q_ref.shape[0]
    tiles = length // TILE
    q, v = q_ref[...], v_ref[...]
    lane = lax.broadcasted_iota(jnp.int32, q.shape, 1)
    keys = jnp.concatenate([k_ref[...], segk_ref[...]], axis=1)
    halves = []
    for h in range(2):
        mine = (lane < HEAD_DIM) if h == 0 else (lane >= HEAD_DIM)
        queries = jnp.concatenate([jnp.where(mine, q, jnp.zeros_like(q)), segq_ref[...]], axis=1)
        s_ref[h] = nt(queries, keys)
    for h in range(2):
        below = table_ref[15, 2 * pair + h]
        above = table_ref[31, 2 * pair + h]
        for r in range(0, length, CHUNK):
            t = r // TILE
            parts = []
            for u in range(tiles):
                d = u - t
                part = s_ref[h, r : r + CHUNK, u * TILE : (u + 1) * TILE]
                if abs(d) <= 1:
                    part = part + band_ref[h, r - t * TILE : r - t * TILE + CHUNK, (d + 1) * TILE : (d + 2) * TILE]
                else:
                    part = part + (above if d > 0 else below)
                parts.append(part)
            s = jnp.concatenate(parts, axis=1)
            p = jnp.exp(s - jnp.max(s, axis=-1, keepdims=True))
            p = p * (1.0 / jnp.sum(p, axis=-1, keepdims=True))
            probs_ref[h, r : r + CHUNK, :] = p.astype(BF16)
        halves.append(nn(probs_ref[h], v))
    ctx_ref[...] = jnp.where(lane < HEAD_DIM, halves[0], halves[1]).astype(BF16)


def out_kernel(pattern, where, x_ref, ctx_a_ref, ctx_b_ref, gains_ref, perm_ref, *refs):
    count = len(pattern) + 1 if pattern else 1
    attn_ref, second_ref, second_t_ref = refs[count : count + 3]
    if pattern:
        w_ref, hold_ref = refs[count + 3 : count + 5]
        fill_rows(where, pattern, refs[:count], hold_ref, refs[1].shape[1] - refs[0].shape[0] // 4)
        w_ref[...] = hold_ref[...].astype(BF16)
    else:
        w_ref = refs[0]
    ctx = jnp.concatenate([ctx_a_ref[...], ctx_b_ref[...]], axis=1)
    attn = nn(ctx, w_ref[...])
    attn_ref[...] = attn
    middle = x_ref[...].astype(F32) + attn
    r2 = lax.rsqrt(jnp.mean(middle * middle, axis=-1, keepdims=True) + EPS)
    second = (middle * r2 * gains_ref[1:]).astype(BF16)
    second_ref[...] = second
    second_t_ref[...] = nt(perm_ref[...], second).astype(BF16)


def up_kernel(pattern, place, where, second_ref, keep_ref, mate_ref, away_ref, far_ref, *refs):
    glow_ref = refs[-1]
    refs = refs[:-1]

    @pl.when(pl.program_id(0) == 0)
    def _():
        row_of(where, (keep_ref, mate_ref, away_ref, far_ref), glow_ref)

    if pattern:
        w_ref = refs[-1]

        @pl.when(pl.program_id(0) == 0)
        def _():
            fill(where, pattern, refs[: len(pattern) + 1], w_ref, False)

        weight = w_ref[pl.program_id(0)]
        act_ref, slope_ref, wd_keep_ref, wd_send_ref = refs[len(pattern) + 1 : len(pattern) + 5]
        weight = weight.reshape(-1, weight.shape[-1])
    else:
        weight = flat(refs[0])
        act_ref, slope_ref, wd_keep_ref, wd_send_ref = refs[1:]
    up = nn(second_ref[...], weight)
    phi_cap = 0.5 * (1.0 + lax.erf(up * 0.7071067811865476))
    act = (up * phi_cap).astype(BF16)
    act_ref[...] = act
    slope = phi_cap + up * (jnp.exp(-0.5 * up * up) * 0.3989422804014327)
    slope_ref[...] = slope.astype(BF16)
    dwd = tn(act, flat(glow_ref))
    if len(wd_keep_ref.shape) == 2:
        wd_keep_ref[...] = dwd.astype(BF16)
    else:
        rows = wd_keep_ref.shape[-2]
        blocks = [dwd[i * rows : (i + 1) * rows].astype(BF16) for i in range(8)]
        for axis, bit in ((1, 4), (2, 2), (3, 1)):
            flip = place[axis] == 1
            blocks = [jnp.where(flip, blocks[i ^ bit], blocks[i]) for i in range(8)]
        core = place[3]
        for ref, c_rel in ((wd_keep_ref, 0), (wd_send_ref, 1)):
            x_outer = core == c_rel
            for i in range(2):
                for j in range(2):
                    one, other = blocks[4 * i + 2 * j + c_rel], blocks[4 * j + 2 * i + c_rel]
                    ref[i, j, 0, 0] = one if i == j else jnp.where(x_outer, one, other)


def down_kernel(pattern, where, second_t_ref, glow_ref, attn_ref, act_ref, slope_ref, win_ref, *refs):
    j = pl.program_id(0)
    win = flat(win_ref)
    count = len(pattern) + 1 if pattern else 1
    keep_ref, mate_ref, away_ref, dsec_ref, win_keep_ref, win_send_ref, acc_ref, dacc_ref, hold_ref = refs[count : count + 9]
    if pattern:
        w_ref = refs[-1]

        @pl.when(j == 0)
        def _():
            fill(where, pattern, refs[:count], w_ref, True)

        shards = w_ref.shape[0] // 4
        wd = w_ref[pl.ds(j * shards, shards)]
        wd = wd.reshape(-1, wd.shape[-1])
    else:
        wd = flat(refs[0])
    gup = (nt(glow_ref[...], wd) * slope_ref[...].astype(F32)).astype(BF16)
    out = nn(act_ref[...], wd)
    dsec = nt(gup, win)

    @pl.when(j == 0)
    def _():
        acc_ref[...] = attn_ref[...] + out
        dacc_ref[...] = dsec

    @pl.when(j > 0)
    def _():
        acc_ref[...] += out
        dacc_ref[...] += dsec

    @pl.when(j == pl.num_programs(0) - 1)
    def _():
        place_rows(where, acc_ref[...], keep_ref, mate_ref, away_ref, hold_ref)
        dsec_ref[...] = dacc_ref[...]

    dwin = nn(second_t_ref[...], gup).astype(BF16)
    half = dwin.shape[0] // 2
    win_keep_ref[...] = dwin[:half]
    win_send_ref[...] = dwin[half:]


def mid_kernel(
    x_ref, attn_ref, gains_ref, dsec_ref, glow_ref, ctx_a_ref, ctx_b_ref, perm_ref, w_ref,
    gmd_ref, g2_ref, dctx_ref, keep_ref, send_ref,
):
    middle = x_ref[...].astype(F32) + attn_ref[...]
    r2 = lax.rsqrt(jnp.mean(middle * middle, axis=-1, keepdims=True) + EPS)
    normed = middle * r2
    dsec = dsec_ref[...]
    g2_ref[...] = jnp.sum(dsec * normed, axis=0, keepdims=True)
    scaled = dsec * gains_ref[1:]
    gmd = r2 * (scaled - normed * jnp.mean(scaled * normed, axis=-1, keepdims=True))
    gmd_ref[...] = gmd
    low = (glow_ref[...].astype(F32) + gmd).astype(BF16)
    dctx_ref[...] = nt(low, w_ref[...]).astype(BF16)
    ctx_t = nt(perm_ref[...], jnp.concatenate([ctx_a_ref[...], ctx_b_ref[...]], axis=1)).astype(BF16)
    dw = nn(ctx_t, low).astype(BF16)
    half = dw.shape[0] // 2
    keep_ref[...] = dw[:half]
    send_ref[...] = dw[half:]


def back_kernel(q_ref, k_ref, v_ref, dctx_ref, ctx_ref, probs_ref, dq_ref, dk_ref, dv_ref, sums_ref, ds_ref, dp_ref, near_ref):
    length = q_ref.shape[0]
    tiles = length // TILE
    q, k, v, dctx = q_ref[...], k_ref[...], v_ref[...], dctx_ref[...]
    lane = lax.broadcasted_iota(jnp.int32, (length, TILE), 1)
    product = dctx.astype(F32) * ctx_ref[...].astype(F32)
    square = lambda axis: lax.broadcasted_iota(jnp.int32, (TILE, TILE), axis)
    turn = (square(0) + square(1) == TILE - 1).astype(F32)
    row = lax.broadcasted_iota(jnp.int32, (TILE, 3 * TILE), 0)
    column = lax.broadcasted_iota(jnp.int32, (TILE, 3 * TILE), 1)
    dqs, dk, dv = [], None, None

    def put(old, new):
        return new if old is None else old + new

    masked = []
    for h in range(2):
        mine = (lane < HEAD_DIM) if h == 0 else (lane >= HEAD_DIM)
        do = jnp.where(mine, dctx, jnp.zeros_like(dctx))
        dp_ref[h] = nt(do, v)
        masked.append((mine, do))
    for h in range(2):
        mine, do = masked[h]
        delta = jnp.sum(jnp.where(mine, product, 0.0), axis=-1, keepdims=True)
        far = [None, None]
        for start in range(0, TILE, CHUNK):
            band = [None, None, None]
            for t in range(tiles):
                rows = slice(t * TILE + start, t * TILE + start + CHUNK)
                ds = probs_ref[h, rows, :].astype(F32) * (dp_ref[h, rows, :] - delta[rows])
                ds_ref[h, rows, :] = ds.astype(BF16)
                for u in range(tiles):
                    d = u - t
                    part = ds[:, u * TILE : (u + 1) * TILE]
                    if abs(d) <= 1:
                        band[d + 1] = put(band[d + 1], part)
                    else:
                        far[int(d > 0)] = put(far[int(d > 0)], part)
            near_ref[start : start + CHUNK, :] = jnp.concatenate(band, axis=1)
        near = near_ref[...]
        outside = jnp.where(column < row, near, 0.0)
        near = jnp.where(column < row, 0.0, near)
        near = lax.dot_general(turn, near, (((1,), (0,)), ((), ())), precision=HIGHEST, preferred_element_type=F32)
        near = pltpu.roll(near, 0, 1, stride=1, stride_axis=0)
        sums_ref[0, h : h + 1, :] = jnp.sum(near, axis=0, keepdims=True)
        sums_ref[0, 2 + h : 3 + h, :] = jnp.sum(outside, axis=0, keepdims=True)
        for i in range(2):
            sums_ref[0, 4 + 2 * i + h : 5 + 2 * i + h, :TILE] = jnp.sum(far[i], axis=0, keepdims=True)
            sums_ref[0, 4 + 2 * i + h : 5 + 2 * i + h, TILE:] = jnp.zeros((1, 2 * TILE), F32)
        dqs.append(nn(ds_ref[h], k))
        dk = put(dk, tn(ds_ref[h], jnp.where(mine, q, jnp.zeros_like(q))))
        dv = put(dv, tn(probs_ref[h], do))
    dq_ref[...] = jnp.where(lane < HEAD_DIM, dqs[0], dqs[1]).astype(BF16)
    dk_ref[...] = dk.astype(BF16)
    dv_ref[...] = dv.astype(BF16)


def grad_kernel(dqa_ref, dqb_ref, dka_ref, dkb_ref, dva_ref, dvb_ref, first_t_ref, keep_ref, send_ref):
    refs = (dqa_ref, dqb_ref, dka_ref, dkb_ref, dva_ref, dvb_ref)
    dw = nn(first_t_ref[...], jnp.concatenate([ref[...] for ref in refs], axis=1)).astype(BF16)
    half = dw.shape[0] // 2
    keep_ref[...] = dw[:half]
    send_ref[...] = dw[half:]


def first_kernel(
    where, x_ref, gains_ref, dqa_ref, dqb_ref, dka_ref, dkb_ref, dva_ref, dvb_ref, w_ref, gmd_ref,
    g2_ref, sums_a_ref, sums_b_ref, row_keep_ref, row_mate_ref, row_away_ref, small_ref, hold_ref,
):
    width = x_ref.shape[1]
    x = x_ref[...].astype(F32)
    r1 = lax.rsqrt(jnp.mean(x * x, axis=-1, keepdims=True) + EPS)
    normed = x * r1
    refs = (dqa_ref, dqb_ref, dka_ref, dkb_ref, dva_ref, dvb_ref)
    dfirst = times_transposed(jnp.concatenate([ref[...] for ref in refs], axis=1), w_ref, 0, 3 * width)
    lines = width // TILE
    for i, gain_grad in enumerate((jnp.sum(dfirst * normed, axis=0, keepdims=True), g2_ref[...])):
        for k in range(lines):
            small_ref[i * lines + k : i * lines + k + 1, :] = gain_grad[:, k * TILE : (k + 1) * TILE]
    picked = [[], [], []]
    for ref in (sums_a_ref, sums_b_ref):
        for p in range(ref.shape[0]):
            picked[0].append(ref[p, 0:2])
            picked[1].append(ref[p, 2:4] + ref[p, 4:6])
            picked[2].append(ref[p, 6:8])
    near, below, above = (jnp.concatenate(part, axis=0) for part in picked)
    square = (3 * TILE, TILE)
    offset = lax.broadcasted_iota(jnp.int32, square, 0) - (TILE - 1)
    offset = jnp.where(offset < 0, offset + 3 * TILE, offset) - TILE
    bucket = lax.broadcasted_iota(jnp.int32, square, 1)
    choice = (bucket_of(offset) == bucket).astype(F32)
    table = lax.dot_general(near, choice, (((1,), (0,)), ((), ())), precision=HIGHEST, preferred_element_type=F32)
    lane = lax.broadcasted_iota(jnp.int32, table.shape, 1)
    table = table + jnp.where(lane == 15, jnp.sum(below, axis=-1, keepdims=True), 0.0)
    table = table + jnp.where(lane == 31, jnp.sum(above, axis=-1, keepdims=True), 0.0)
    small_ref[2 * lines : 2 * lines + HEADS, :] = table
    scaled = dfirst * gains_ref[:1]
    delta = gmd_ref[...] + r1 * (scaled - normed * jnp.mean(scaled * normed, axis=-1, keepdims=True))
    place_rows(where, delta, row_keep_ref, row_mate_ref, row_away_ref, hold_ref)


def shape(dims, dtype):
    return jax.ShapeDtypeStruct(tuple(dims), dtype)


def after(value, *earlier):
    return lax.optimization_barrier((value,) + earlier)[0]


def total(*parts):
    sums = parts[0].astype(F32)
    for part in parts[1:]:
        sums = sums + part.astype(F32)
    return sums


def on_device(
    nb, ns, hidden_in, doc_lengths, bias_table, gain_attn, gain_ffn,
    w_query, w_key, w_value, w_out, w_in, w_down, out_grad,
):
    rows_dev, shard_len, width = hidden_in.shape
    length = ns * shard_len
    ff = w_in.shape[1]
    shard = w_query.shape[0]
    b, s = lax.axis_index("batch"), lax.axis_index("seq")
    y, c = s // 2, s % 2
    bits = [1 << i for i in range(1, nb.bit_length() - 1)]
    gather_order = ([1] + bits[::-1], bits[::-1] + [1])

    def masks(core):
        value = [0]
        for bit in gather_order[core]:
            value = value + [old ^ bit for old in value]
        return value

    where = jnp.concatenate([jnp.stack([b, s]), jnp.array(masks(0) + masks(1))]).astype(jnp.int32)

    def move(value, first, second=None):
        pairs = []
        for i in range(nb):
            for j in range(ns):
                bm, sm = second if second is not None and j % 2 else first
                pairs.append((i * ns + j, (i ^ bm) * ns + (j ^ sm)))
        return lax.ppermute(value, ("batch", "seq"), pairs)

    core = lambda value: move(value, (0, 1))
    other_y = lambda value: move(value, (0, 2))

    def piece(weight, parts, axis=1):
        size = weight.shape[axis] // parts
        return lax.dynamic_slice_in_dim(weight, (c if parts == 2 else s) * size, size, axis)[None]

    def step(block, i):
        return move(block, (gather_order[0][i], 0), (gather_order[1][i], 0))

    tiled = (shard // 2) % 16 == 0

    def plain(local, pieces, axis=1, low=0, high=None):
        parts = 4 if any(entry[1] > 1 for entry in pieces) else 2
        own = jnp.stack(jnp.split(local, parts, axis))
        full = jnp.zeros((parts, nb) + own.shape[1:], BF16).at[:, b].set(own)
        for array, flip, base in pieces:
            part = s ^ flip if parts == 4 else (s ^ flip) % 2
            shards = b ^ jnp.where((s ^ flip) % 2 == 0, jnp.array(masks(0)), jnp.array(masks(1)))
            full = full.at[part, shards[base : base + array.shape[0]]].set(array[:, low:high])
        if axis == 0:
            return jnp.swapaxes(full, 0, 1)
        return full.reshape(parts, 1, -1, own.shape[2])

    class Gather:
        def __init__(self, block):
            self.block, self.brought = block, []

        def start(self):
            self.brought.append(step(self.block, len(self.brought)))
            return self.brought[-1]

        def grow(self, *gates):
            self.brought[-1] = after(self.brought[-1], *gates) if gates else self.brought[-1]
            self.block = jnp.concatenate([self.block, self.brought[-1]])
            return self.block

    vmem = pl.BlockSpec(memory_space=pltpu.VMEM)
    smem = pl.BlockSpec(memory_space=pltpu.SMEM)
    stages = len(bits) + 1

    per = width // (nb * ns)
    feature = jnp.arange(width)
    fb, fs, fr = feature // (per * ns), feature // per % ns, feature % per
    b_rel, s_rel = fb ^ b, fs ^ s
    x_rel, y_rel = b_rel % 2, s_rel // 2
    swapped = fs % 2 == 1
    position = (s_rel % 2) * 2 + jnp.where(swapped, y_rel, x_rel)
    position = position * 2 + jnp.where(swapped, x_rel, y_rel)
    for bit in bits:
        position = position * 2 + (b_rel & bit) // bit
    position = (position * per + fr).reshape(1, width)

    own = jnp.zeros((2, width), BF16)
    own = lax.dynamic_update_slice(own, jnp.stack([gain_attn, gain_ffn]), (0, b * shard)).reshape(-1, TILE)
    own = jnp.pad(own, ((0, shard - own.shape[0]), (0, TILE)))
    local1 = jnp.concatenate([w_query, w_key, w_value, own], axis=1)
    one = Gather(piece(local1, 4))
    one.start()
    row_shapes = (shape((shard_len, width), BF16),) * 2 + (shape((2, shard_len, width), BF16),)
    row_keep, row_mate, row_away, grad_keep, grad_mate, grad_away = pl.pallas_call(
        pack_kernel,
        name="pack",
        out_shape=row_shapes * 2,
        in_specs=[smem, vmem, vmem],
        cost_estimate=cost(3),
        compiler_params=params(),
    )(where, hidden_in, out_grad)
    row_got = other_y(row_away)
    band, seg_queries, seg_keys, perm = pl.pallas_call(
        prepare_kernel,
        name="prepare",
        out_shape=(
            shape((HEADS, TILE, 3 * TILE), F32), shape((length, TILE), BF16), shape((length, TILE), BF16),
            shape((width, width), BF16),
        ),
        in_specs=[smem, smem, smem, vmem],
        cost_estimate=cost(6),
        compiler_params=params(),
    )(where, doc_lengths, bias_table, position)
    def tagged(arrays, flip):
        return [(array, flip, 1 << i) for i, array in enumerate(arrays)]

    y_one = [other_y(one.brought[0])]
    while len(one.brought) < stages - 1:
        one.grow()
        one.start()
        if len(one.brought) < stages - 1:
            y_one.append(other_y(one.brought[-1]))
    one.grow(band, row_got, *y_one)
    one.start()
    y_one.append(other_y(one.brought[-2]))
    core_one = [core(array) for array in one.brought[:-1]]
    two = Gather(jnp.concatenate([piece(after(w_in, one.block), 4), piece(w_out, 4, 0)], axis=1))
    two.start()
    one.brought[-1] = after(one.brought[-1], *y_one, *core_one)
    core_one.append(core(one.brought[-1]))
    y_one.append(after(other_y(one.brought[-1]), two.brought[0]))
    row_mate, row_far = core(row_mate), core(row_got[1])
    while len(two.brought) < stages - 1:
        two.grow()
        two.start()
    two.grow()
    y_two = [other_y(after(array, y_one[-1])) for array in two.brought]
    two.start()
    three = Gather(piece(after(w_down, two.block), 2, 0))
    three.start()
    gather1 = tagged(one.brought, 0) + tagged(core_one, 1) + tagged(y_one, 2) + tagged([core(array) for array in y_one], 3)
    part = ff // 4

    row_block = shape((4, shard_len, width), BF16)
    w1_shape = shape((4, nb) + one.block.shape[1:], BF16)
    pieces1 = [local1] + [entry[0] for entry in gather1] if tiled else [plain(local1, gather1)]
    outputs = pl.pallas_call(
        functools.partial(qkv_kernel, [entry[1:] for entry in gather1] if tiled else None, shard),
        name="qkv",
        out_shape=(
            shape((length, 3 * width), BF16), shape((width, length), BF16), row_block, shape((2, width), F32),
            *([w1_shape] if tiled else []),
        ),
        in_specs=[smem] + [vmem] * (5 + len(pieces1)),
        cost_estimate=cost(9),
        compiler_params=params(),
    )(where, row_keep, row_mate, row_got, row_far, perm, after(pieces1[0], two.block, three.block), *pieces1[1:])
    qkv, first_t, xb, gains = outputs[:4]
    w1 = outputs[4] if tiled else pieces1[0]
    xb = xb.reshape(length, width)

    two.brought[-1] = after(two.brought[-1], qkv)
    y_two.append(other_y(two.brought[-1]))
    grad_got = other_y(after(grad_away, two.brought[-1]))
    while len(three.brought) < stages - 2:
        three.grow(qkv)
        three.start()
    three.grow(qkv)

    pairs = HEADS // 4
    pair_block = lambda first: pl.BlockSpec((length, TILE), lambda p: (0, first + p))
    head_block = lambda first, *dims: pl.BlockSpec((2,) + dims, lambda p: (first + p,) + (0,) * len(dims))
    whole_block = lambda *dims: pl.BlockSpec(dims, lambda p: (0,) * len(dims))

    def attend(i, gated):
        return pl.pallas_call(
            functools.partial(attention_kernel, i * pairs),
            name="attention",
            grid=(pairs,),
            out_shape=(shape((HEADS // 2, length, length), BF16), shape((length, width // 2), BF16)),
            in_specs=[
                pair_block(i * pairs), pair_block((2 + i) * pairs), pair_block((4 + i) * pairs),
                head_block(i * pairs, TILE, 3 * TILE), smem, whole_block(length, TILE), whole_block(length, TILE),
            ],
            out_specs=(head_block(0, length, length), pair_block(0)),
            scratch_shapes=[pltpu.VMEM((2, length, length), F32)],
            cost_estimate=cost(10),
            compiler_params=params(),
        )(qkv, qkv, qkv, gated, bias_table, seg_queries, seg_keys)

    probs_a, ctx_a = attend(0, after(band, two.brought[-1], three.block, *y_two[:-1]))
    probs_b, ctx_b = attend(1, after(band, ctx_a))
    three.start()
    three.grow(ctx_b)
    y_two_core = [core(after(array, ctx_b)) for array in y_two]
    gather2 = tagged(two.brought, 0) + tagged([core(array) for array in two.brought], 1) + tagged(y_two, 2) + tagged(y_two_core, 3)
    pattern2 = [entry[1:] for entry in gather2]
    arrays2 = [entry[0] for entry in gather2]
    if tiled:
        wo_pieces = [w_out] + arrays2
    else:
        wo_pieces = [plain(w_out, gather2, 0, shard).reshape(width, width)]
    outputs = pl.pallas_call(
        functools.partial(out_kernel, pattern2 if tiled else None),
        name="out",
        out_shape=(
            shape((length, width), F32), shape((length, width), BF16), shape((width, length), BF16),
            *([shape((width, width), BF16)] if tiled else []),
        ),
        in_specs=[smem] + [vmem] * (5 + len(wo_pieces)),
        scratch_shapes=[pltpu.VMEM((width, width), F32)] if tiled else [],
        cost_estimate=cost(6),
        compiler_params=params(),
    )(where, xb, after(ctx_a, three.block), ctx_b, gains, perm, *wo_pieces)
    attn, second, second_t = outputs[:3]
    wo = outputs[3] if tiled else wo_pieces[0]
    high3 = three.start()
    grad_got = after(grad_got, second)
    grad_mate, grad_far = core(after(grad_mate, ctx_b)), core(grad_got[1])
    gather3 = tagged(three.brought, 0) + tagged([core(array) for array in three.brought], 1)

    steps = 4
    per_down = ff // (nb * ns)
    aligned = nb == 2 * steps and per_down % 16 == 0
    if aligned:

        def wd_index(j, place):
            rel = j ^ place[0]
            return 0, 0, rel % 2, rel // 2, 0, 0

        wd_block = pl.BlockSpec((2, 2, 1, 1, per_down, width), wd_index)
        wd_shape = shape((2, 2, 2, 2, per_down, width), BF16)
        wd_shapes, wd_blocks = (wd_shape, wd_shape), (wd_block, wd_block)
    else:
        wd_shapes = (shape((ff, width), BF16), shape((8, TILE), BF16))
        wd_blocks = (
            pl.BlockSpec((part, width), lambda j, place: (j, 0)),
            pl.BlockSpec((8, TILE), lambda j, place: (0, 0)),
        )
    place = jnp.stack([b // 2, b % 2, y, c]).astype(jnp.int32)
    full = lambda *dims: pl.BlockSpec(dims, lambda j, *place: (0,) * len(dims))
    row_specs = (full(shard_len, width), full(shard_len, width), full(2, shard_len, width))
    half = width // 2
    column_block = lambda r: pl.BlockSpec((r, part), lambda j, *place: (0, j))
    win_shape = (4, nb, shard, part)
    pieces2 = [w_in] + arrays2 if tiled else [plain(w_in, gather2, 1, 0, shard)]
    win_shape = win_shape if tiled else pieces2[0].shape
    win_block = pl.BlockSpec((1,) + win_shape[1:], lambda j, *place: (j, 0, 0, 0))
    always = lambda array: pl.BlockSpec(array.shape, lambda j, *place: (0,) * array.ndim)
    outputs = pl.pallas_call(
        functools.partial(up_kernel, pattern2 if tiled else None),
        name="up",
        out_shape=(
            shape((length, ff), BF16), shape((length, ff), BF16), *wd_shapes, *([shape(win_shape, BF16)] if tiled else []), row_block,
        ),
        grid_spec=pltpu.PrefetchScalarGridSpec(
            num_scalar_prefetch=1,
            grid=(steps,),
            in_specs=[smem, full(length, width), *row_specs[:2], row_specs[2], row_specs[0]]
            + ([always(array) for array in pieces2] if tiled else [win_block]),
            out_specs=(
                column_block(length), column_block(length), *wd_blocks, *([full(*win_shape)] if tiled else []), full(*row_block.shape),
            ),
        ),
        cost_estimate=cost(10),
        compiler_params=params(),
    )(place, where, second, grad_keep, grad_mate, grad_got, grad_far, *pieces2)
    act, slope, wd_keep, wd_send = outputs[:4]
    win = outputs[4] if tiled else pieces2[0]
    glow = outputs[-1].reshape(length, width)

    scatter_masks = [((1, 0), (0, 2)), ((0, 2), (1, 0))] + [((bit, 0), (bit, 0)) for bit in bits]

    class Scatter:
        def __init__(self, *held):
            self.held = [value if isinstance(value, tuple) else (value,) for value in held]
            self.rows = self.held[0][0].shape[0]
            self.widths = [value.shape[1] for value in self.held[0]]
            self.i = 0

        def outgoing(self):
            rows = slice(self.rows // 2, self.rows)
            groups = [total(*[value[rows] for value in group]).astype(BF16) for group in zip(*self.held)]
            self.sent = groups[0] if len(groups) == 1 else jnp.concatenate(groups, axis=1)
            return self.sent

        def send(self):
            self.got = move(self.sent, *scatter_masks[self.i])

        def take(self, *gates):
            self.i += 1
            self.rows //= 2
            got = after(self.got, *gates)
            starts = [sum(self.widths[:k]) for k in range(len(self.widths))]
            self.held.append(tuple(got[:, low : low + size] for low, size in zip(starts, self.widths)))

        def result(self):
            groups = [total(*[value[: self.rows] for value in group]) for group in zip(*self.held)]
            return groups[0] if len(groups) == 1 else groups

    if not aligned:
        blocks = wd_keep.reshape(nb, ns, per_down, width)

        def order(dest):
            index = jnp.arange(nb * 2)
            digits = [(index >> (stages - i)) % 2 for i in range(stages + 1)]
            x_bit = jnp.where(dest == 0, digits[0], digits[1])
            y_bit = jnp.where(dest == 0, digits[1], digits[0])
            shards = x_bit
            for bit, digit in zip(bits, digits[2:]):
                shards = shards + bit * digit
            return blocks[shards ^ b, 2 * (y_bit ^ y) + dest]

        wd_keep, wd_send = order(c), order(1 - c)
    wd_keep, wd_send = wd_keep.reshape(ff // 2, width), wd_send.reshape(ff // 2, width)
    down = Scatter(wd_keep, core(after(wd_send, high3)))
    down_sent = down.outgoing()
    down.send()

    pieces3 = [w_down] + [entry[0] for entry in gather3] if tiled else [plain(w_down, gather3, 0)]
    wd_dims = (nb, 2) + three.block.shape[1:]
    wd_spec = pl.BlockSpec((nb // steps,) + wd_dims[1:], lambda j: (j, 0, 0, 0))
    hold = pltpu.VMEM((4, shard_len, width), BF16)
    out_keep, out_mate, out_away, dsec, win_keep, win_send = pl.pallas_call(
        functools.partial(down_kernel, [entry[1:] for entry in gather3] if tiled else None),
        name="down",
        grid=(steps,),
        out_shape=(*row_shapes, shape((length, width), F32), shape((half, ff), BF16), shape((half, ff), BF16)),
        in_specs=[
            smem, full(width, length), full(length, width), full(length, width), column_block(length),
            column_block(length), win_block, *([always(array) for array in pieces3] if tiled else [wd_spec]),
        ],
        out_specs=(*row_specs, full(length, width), column_block(half), column_block(half)),
        scratch_shapes=[
            pltpu.VMEM((length, width), F32), pltpu.VMEM((length, width), F32), hold,
            *([pltpu.VMEM(wd_dims, BF16)] if tiled else []),
        ],
        cost_estimate=cost(15),
        compiler_params=params(),
    )(where, second_t, glow, attn, after(act, down_sent), slope, win, *pieces3)
    win_got = core(win_send)
    down.take(dsec)
    down_sent = down.outgoing()
    down.send()
    out_got = other_y(out_away)

    gmd, g2, dctx, wo_keep, wo_send = pl.pallas_call(
        mid_kernel,
        name="mid",
        out_shape=(
            shape((length, width), F32), shape((1, width), F32), shape((length, width), BF16),
            shape((half, width), BF16), shape((half, width), BF16),
        ),
        cost_estimate=cost(7),
        compiler_params=params(),
    )(xb, attn, gains, after(dsec, down_sent), glow, ctx_a, ctx_b, perm, wo)
    wo_got = core(wo_send)
    both = Scatter((win_keep, wo_keep), (after(win_got, dctx), wo_got))
    both_sent = both.outgoing()
    both.send()
    down.take(dctx)
    down_sent = down.outgoing()
    down.send()

    def back(i, gated):
        return pl.pallas_call(
            back_kernel,
            name="back",
            grid=(pairs,),
            out_shape=(*(shape((length, width // 2), BF16),) * 3, shape((pairs, 8, 3 * TILE), F32)),
            in_specs=[
                pair_block(i * pairs), pair_block((2 + i) * pairs), pair_block((4 + i) * pairs),
                pair_block(i * pairs), pair_block(0), head_block(0, length, length),
            ],
            out_specs=(*(pair_block(0),) * 3, pl.BlockSpec((1, 8, 3 * TILE), lambda p: (p, 0, 0))),
            scratch_shapes=[
                pltpu.VMEM((2, length, length), BF16), pltpu.VMEM((2, length, length), F32), pltpu.VMEM((TILE, 3 * TILE), F32),
            ],
            cost_estimate=cost(10),
            compiler_params=params(),
        )(qkv, qkv, qkv, gated, (ctx_a, ctx_b)[i], (probs_a, probs_b)[i])

    dq_a, dk_a, dv_a, sums_a = back(0, after(dctx, down_sent, both_sent))
    down.take(dq_a)
    down_sent = down.outgoing()
    down.send()
    dq_b, dk_b, dv_b, sums_b = back(1, after(dctx, down_sent))
    both.take(dq_b)
    both_sent = both.outgoing()
    both.send()

    grads = (after(dq_a, both_sent), dq_b, dk_a, dk_b, dv_a, dv_b)
    keep, send = pl.pallas_call(
        grad_kernel,
        name="grad",
        out_shape=(shape((half, 3 * width), BF16),) * 2,
        cost_estimate=cost(5),
        compiler_params=params(),
    )(*grads, first_t)
    last_got = core(send)
    both.take(send)
    both_sent = both.outgoing()
    both.send()
    last = Scatter(keep, after(last_got, both_sent))
    last_sent = last.outgoing()
    last.send()
    small_lines = 2 * width // TILE
    in_keep, in_mate, in_away, small = pl.pallas_call(
        first_kernel,
        name="first",
        out_shape=(*row_shapes, shape((small_lines + HEADS, TILE), F32)),
        in_specs=[smem] + [vmem] * 13,
        scratch_shapes=[hold],
        cost_estimate=cost(7),
        compiler_params=params(),
    )(where, xb, gains, after(grads[0], last_sent), *grads[1:], w1, gmd, g2, sums_a, sums_b)
    last.got = after(last.got, both.got)
    in_got = other_y(after(in_away, last.got))
    small = after(small, last.got)
    last.take()
    last_sent = last.outgoing()
    last.send()
    op2_sent = last_sent
    both.take(last_sent)
    while both.i < stages:
        both.outgoing()
        both.send()
        both.take()
    both.outgoing()
    both.send()

    def unpack(name, old, keep, mate, got):
        mate, far = core(after(mate, got)), core(got[1])
        return pl.pallas_call(
            unpack_kernel,
            name=name,
            out_shape=shape(old.shape, F32),
            in_specs=[smem] + [vmem] * 5,
            cost_estimate=cost(3),
            compiler_params=params(),
        )(where, old, keep, mate, got, far)

    out_hidden = unpack("out_rows", hidden_in, out_keep, out_mate, after(out_got, op2_sent))
    small = small + move(small, (0, 1))
    small = small + move(after(small, op2_sent), (1, 0))
    last.take(out_hidden, small)
    last.outgoing()
    last.send()
    both.take(last.sent)
    down.take(last.sent)
    while down.i < stages + 1:
        down.outgoing()
        down.send()
        down.take()
    input_grad = unpack("in_rows", out_grad, in_keep, in_mate, after(in_got, last.sent))
    for bit in bits[:-1]:
        small = small + move(after(small, last.sent), (bit, 0))
    small = small + move(small, (0, 2))
    last.take(input_grad, small)
    last_sent = last.outgoing()
    last.send()
    small = small + move(after(small, last_sent), (bits[-1], 0))
    last.take()
    while last.i < stages + 1:
        last.outgoing()
        last.send()
        last.take()
    down_grad_w = down.result()
    both_sum, last_sum = both.result(), last.result()
    gain_grads = small[:small_lines].reshape(2, width)
    gain_grads = lax.dynamic_slice_in_dim(gain_grads, (b * ns + s) * per, per, 1)
    table = small[small_lines:, :BUCKETS].T

    return (
        out_hidden,
        input_grad,
        table,
        gain_grads[0],
        gain_grads[1],
        last_sum[:, :width],
        last_sum[:, width : 2 * width],
        last_sum[:, 2 * width :],
        both_sum[1],
        both_sum[0],
        down_grad_w,
    )


def solution(mesh):
    nb, ns = mesh.shape["batch"], mesh.shape["seq"]
    placed = (
        P("batch", "seq", None),
        P("batch", None),
        P(),
        P("batch"),
        P("batch"),
        P("batch", None),
        P("batch", None),
        P("batch", None),
        P("batch", None),
        P("batch", None),
        P("batch", None),
        P("batch", "seq", None),
    )
    both = ("batch", "seq")
    return jax.shard_map(
        functools.partial(on_device, nb, ns),
        mesh=mesh,
        in_specs=placed,
        out_specs=(
            P("batch", "seq", None),
            P("batch", "seq", None),
            P(),
            P(both),
            P(both),
            P(both, None),
            P(both, None),
            P(both, None),
            P(both, None),
            P(both, None),
            P(both, None),
        ),
        check_vma=False,
    )
```

```python
import functools

import jax
import jax.numpy as jnp
from jax import lax
from jax.experimental import pallas as pl
from jax.experimental.pallas import tpu as pltpu
from jax.sharding import PartitionSpec as P

HEADS = 12
HEAD_DIM = 64
BUCKETS = 32
TILE = 128

EPS = 1e-06
THRESHOLDS = (12, 16, 23, 32, 46, 64, 91)
HIGHEST = lax.Precision.HIGHEST
F32 = jnp.float32
BF16 = jnp.bfloat16
VMEM_LIMIT = 56 * 1024 * 1024


def bucket_of(offsets):
    distance = jnp.abs(offsets)
    stepped = jnp.full_like(distance, 8)
    for threshold in THRESHOLDS:
        stepped = stepped + (distance >= threshold).astype(jnp.int32)
    closer = jnp.where(distance < 8, distance, stepped)
    return closer + 16 * (offsets > 0).astype(jnp.int32)


def nn(left, right):
    return lax.dot_general(left, right, (((1,), (0,)), ((), ())), preferred_element_type=F32)


def nt(left, right):
    return lax.dot_general(left, right, (((1,), (1,)), ((), ())), preferred_element_type=F32)


def tn(left, right):
    return lax.dot_general(left, right, (((0,), (0,)), ((), ())), preferred_element_type=F32)


def params(**kw):
    return pltpu.CompilerParams(vmem_limit_bytes=VMEM_LIMIT, **kw)


def cost(microseconds):
    return pl.CostEstimate(flops=int(microseconds * 1e9), bytes_accessed=int(microseconds * 3.5e6), transcendentals=0)


def pack_kernel(where, hidden_ref, grad_ref, *refs):
    for source, (keep_ref, mate_ref, away_ref) in ((hidden_ref, refs[:3]), (grad_ref, refs[3:])):
        for rel in range(4):
            target = (keep_ref, mate_ref, away_ref.at[0], away_ref.at[1])[rel]
            target[...] = source[where[1] ^ rel].astype(BF16)


def row_of(where, refs, out):
    for rel in range(4):
        source = (refs[0], refs[1], refs[2].at[0], refs[3])[rel]
        out[where[1] ^ rel] = source[...]


def unpack_kernel(where, old_ref, keep_ref, mate_ref, away_ref, far_ref, new_ref):
    for rel in range(4):
        row = where[1] ^ rel
        source = (keep_ref[...], mate_ref[...], away_ref[0], far_ref[...])[rel]
        new_ref[row] = old_ref[row] + source.astype(F32)


def place_rows(where, value, keep_ref, mate_ref, away_ref, hold_ref):
    size = keep_ref.shape[0]
    hold_ref[...] = value.astype(BF16).reshape(4, size, value.shape[1])
    for rel in range(4):
        target = (keep_ref, mate_ref, away_ref.at[0], away_ref.at[1])[rel]
        target[...] = hold_ref[where[1] ^ rel]


def fill(where, pattern, refs, out, rows_last):
    b, s = where[0], where[1]
    parts, shards = (out.shape[1], out.shape[0]) if rows_last else (out.shape[0], out.shape[1])
    size = out.shape[2] if rows_last else out.shape[3]
    rows = out.shape[2]
    for p in range(parts):
        if rows_last:
            out[b, p] = refs[0][p * size : (p + 1) * size, :]
        else:
            out[p, b] = refs[0][:, p * size : (p + 1) * size]
    for ref, (flip, base) in zip(refs[1:], pattern):
        core = (s ^ flip) % 2
        part = (s ^ flip) if parts == 4 else core
        for i in range(ref.shape[0]):
            t = b ^ where[2 + core * shards + base + i]
            if rows_last:
                out[t, part] = ref[i, :rows, :]
            else:
                out[part, t] = ref[i, :rows, :]


def flat(ref):
    return ref[...].reshape(-1, ref.shape[-1])


def columns_of(w_ref, start, stop):
    size = w_ref.shape[-1]
    pieces = []
    for p in range(w_ref.shape[0]):
        low, high = max(start, p * size), min(stop, (p + 1) * size)
        if low < high:
            value = w_ref[p, :, :, low - p * size : high - p * size]
            pieces.append((value.reshape(-1, high - low), low - start))
    return pieces


def times_columns(left, w_ref, start, stop):
    return jnp.concatenate([nn(left, value) for value, _ in columns_of(w_ref, start, stop)], axis=1)


def times_transposed(left, w_ref, start, stop):
    out = None
    for value, low in columns_of(w_ref, start, stop):
        term = nt(left[:, low : low + value.shape[1]], value)
        out = term if out is None else out + term
    return out


def prepare_kernel(where, lengths, table, position_ref, band_ref, segq_ref, segk_ref, perm_ref):
    s = where[1]
    shape = segq_ref.shape
    token = lax.broadcasted_iota(jnp.int32, shape, 0)
    lane = lax.broadcasted_iota(jnp.int32, shape, 1)
    segment = jnp.zeros(shape, jnp.int32)
    end = 0
    for j in range(lengths.shape[1]):
        end = end + lengths[s, j]
        segment = segment + (token >= end).astype(jnp.int32)
    same = lane == segment
    segq_ref[...] = jnp.where(same, 1.0, 0.0).astype(BF16)
    segk_ref[...] = jnp.where(same | (lane >= lengths.shape[1]), 0.0, -1e30).astype(BF16)
    offset = lax.broadcasted_iota(jnp.int32, (8, 3 * TILE), 1) - TILE
    bucket = bucket_of(offset)
    near = (TILE, 3 * TILE)
    outside = lax.broadcasted_iota(jnp.int32, near, 1) < lax.broadcasted_iota(jnp.int32, near, 0)
    for h in range(band_ref.shape[0]):
        base = jnp.zeros((8, 3 * TILE), F32)
        for i in range(BUCKETS):
            base = jnp.where(bucket == i, table[i, h], base)
        rows = pltpu.roll(jnp.broadcast_to(base[:1], near), 0, 1, stride=1, stride_axis=0)
        band_ref[h] = jnp.where(outside, table[15, h], rows)
    position = lax.broadcasted_iota(jnp.int32, perm_ref.shape, 0)
    perm_ref[...] = jnp.where(position == position_ref[...], 1.0, 0.0).astype(BF16)


def qkv_kernel(pattern, shard, where, keep_ref, mate_ref, away_ref, far_ref, perm_ref, *refs):
    count = len(pattern) + 1 if pattern else 1
    qkv_ref, first_t_ref, x_ref, gains_ref = refs[count : count + 4]
    w_ref = refs[count + 4] if pattern else refs[0]
    if pattern:
        fill(where, pattern, refs[:count], w_ref, False)
    size, width = keep_ref.shape
    row_of(where, (keep_ref, mate_ref, away_ref, far_ref), x_ref)
    gains = gains_of(w_ref, width, shard)
    gains_ref[...] = gains
    x = x_ref[...].reshape(4 * size, width).astype(F32)
    r1 = lax.rsqrt(jnp.mean(x * x, axis=-1, keepdims=True) + EPS)
    first = (x * r1 * gains[:1]).astype(BF16)
    for value, low in columns_of(w_ref, 0, 3 * width):
        qkv_ref[:, low : low + value.shape[1]] = nn(first, value).astype(BF16)
    first_t_ref[...] = nt(perm_ref[...], first).astype(BF16)


def gains_of(w_ref, width, shard):
    size = w_ref.shape[-1]
    spare = w_ref[3 * width // size, :, :, 3 * width % size : 3 * width % size + TILE].astype(F32)
    rows = width // TILE
    if spare.shape[0] > 1:
        together = jnp.sum(spare, axis=0)
        found = [together[k : k + 1] for k in range(2 * rows)]
    else:
        spare = spare.reshape(-1, TILE)
        row = lax.broadcasted_iota(jnp.int32, spare.shape, 0) % shard
        found = [jnp.sum(jnp.where(row == k, spare, 0.0), axis=0, keepdims=True) for k in range(2 * rows)]
    return jnp.concatenate([jnp.concatenate(found[:rows], axis=1), jnp.concatenate(found[rows:], axis=1)], axis=0)


CHUNK = 32


def attention_kernel(first_pair, q_ref, k_ref, v_ref, band_ref, table_ref, segq_ref, segk_ref, probs_ref, ctx_ref, s_ref):
    pair = pl.program_id(0) + first_pair
    length = q_ref.shape[0]
    tiles = length // TILE
    q, v = q_ref[...], v_ref[...]
    lane = lax.broadcasted_iota(jnp.int32, q.shape, 1)
    keys = jnp.concatenate([k_ref[...], segk_ref[...]], axis=1)
    halves = []
    for h in range(2):
        mine = (lane < HEAD_DIM) if h == 0 else (lane >= HEAD_DIM)
        queries = jnp.concatenate([jnp.where(mine, q, jnp.zeros_like(q)), segq_ref[...]], axis=1)
        s_ref[h] = nt(queries, keys)
    for h in range(2):
        below = table_ref[15, 2 * pair + h]
        above = table_ref[31, 2 * pair + h]
        for r in range(0, length, CHUNK):
            t = r // TILE
            parts = []
            for u in range(tiles):
                d = u - t
                part = s_ref[h, r : r + CHUNK, u * TILE : (u + 1) * TILE]
                if abs(d) <= 1:
                    part = part + band_ref[h, r - t * TILE : r - t * TILE + CHUNK, (d + 1) * TILE : (d + 2) * TILE]
                else:
                    part = part + (above if d > 0 else below)
                parts.append(part)
            s = jnp.concatenate(parts, axis=1)
            p = jnp.exp(s - jnp.max(s, axis=-1, keepdims=True))
            p = p * (1.0 / jnp.sum(p, axis=-1, keepdims=True))
            probs_ref[h, r : r + CHUNK, :] = p.astype(BF16)
        halves.append(nn(probs_ref[h], v))
    ctx_ref[...] = jnp.where(lane < HEAD_DIM, halves[0], halves[1]).astype(BF16)


def out_kernel(pattern, where, x_ref, ctx_a_ref, ctx_b_ref, gains_ref, perm_ref, *refs):
    width = x_ref.shape[1]
    count = len(pattern) + 1 if pattern else 1
    attn_ref, second_ref, second_t_ref = refs[count : count + 3]
    if pattern:
        w_ref = refs[count + 3]
        fill(where, pattern, refs[:count], w_ref, False)
    else:
        w_ref = refs[0]
    ctx = jnp.concatenate([ctx_a_ref[...], ctx_b_ref[...]], axis=1)
    attn = times_columns(ctx, w_ref, 0, width)
    attn_ref[...] = attn
    middle = x_ref[...].astype(F32) + attn
    r2 = lax.rsqrt(jnp.mean(middle * middle, axis=-1, keepdims=True) + EPS)
    second = (middle * r2 * gains_ref[1:]).astype(BF16)
    second_ref[...] = second
    second_t_ref[...] = nt(perm_ref[...], second).astype(BF16)


def up_kernel(pattern, place, where, second_ref, keep_ref, mate_ref, away_ref, far_ref, *refs):
    glow_ref = refs[-1]
    refs = refs[:-1]

    @pl.when(pl.program_id(0) == 0)
    def _():
        row_of(where, (keep_ref, mate_ref, away_ref, far_ref), glow_ref)

    if pattern:
        w_ref = refs[-1]

        @pl.when(pl.program_id(0) == 0)
        def _():
            fill(where, pattern, refs[: len(pattern) + 1], w_ref, False)

        weight = w_ref[pl.program_id(0)]
        act_ref, slope_ref, wd_keep_ref, wd_send_ref = refs[len(pattern) + 1 : len(pattern) + 5]
        weight = weight.reshape(-1, weight.shape[-1])
    else:
        weight = flat(refs[0])
        act_ref, slope_ref, wd_keep_ref, wd_send_ref = refs[1:]
    up = nn(second_ref[...], weight)
    phi_cap = 0.5 * (1.0 + lax.erf(up * 0.7071067811865476))
    act = (up * phi_cap).astype(BF16)
    act_ref[...] = act
    slope = phi_cap + up * (jnp.exp(-0.5 * up * up) * 0.3989422804014327)
    slope_ref[...] = slope.astype(BF16)
    dwd = tn(act, flat(glow_ref))
    if len(wd_keep_ref.shape) == 2:
        wd_keep_ref[...] = dwd.astype(BF16)
    else:
        rows = wd_keep_ref.shape[-2]
        blocks = [dwd[i * rows : (i + 1) * rows].astype(BF16) for i in range(8)]
        for axis, bit in ((1, 4), (2, 2), (3, 1)):
            flip = place[axis] == 1
            blocks = [jnp.where(flip, blocks[i ^ bit], blocks[i]) for i in range(8)]
        core = place[3]
        for ref, c_rel in ((wd_keep_ref, 0), (wd_send_ref, 1)):
            x_outer = core == c_rel
            for i in range(2):
                for j in range(2):
                    one, other = blocks[4 * i + 2 * j + c_rel], blocks[4 * j + 2 * i + c_rel]
                    ref[i, j, 0, 0] = one if i == j else jnp.where(x_outer, one, other)


def down_kernel(pattern, where, second_t_ref, glow_ref, attn_ref, act_ref, slope_ref, win_ref, *refs):
    j = pl.program_id(0)
    win = flat(win_ref)
    count = len(pattern) + 1 if pattern else 1
    keep_ref, mate_ref, away_ref, dsec_ref, win_keep_ref, win_send_ref, acc_ref, dacc_ref, hold_ref = refs[count : count + 9]
    if pattern:
        w_ref = refs[-1]

        @pl.when(j == 0)
        def _():
            fill(where, pattern, refs[:count], w_ref, True)

        shards = w_ref.shape[0] // 4
        wd = w_ref[pl.ds(j * shards, shards)]
        wd = wd.reshape(-1, wd.shape[-1])
    else:
        wd = flat(refs[0])
    gup = (nt(glow_ref[...], wd) * slope_ref[...].astype(F32)).astype(BF16)
    out = nn(act_ref[...], wd)
    dsec = nt(gup, win)

    @pl.when(j == 0)
    def _():
        acc_ref[...] = attn_ref[...] + out
        dacc_ref[...] = dsec

    @pl.when(j > 0)
    def _():
        acc_ref[...] += out
        dacc_ref[...] += dsec

    @pl.when(j == pl.num_programs(0) - 1)
    def _():
        place_rows(where, acc_ref[...], keep_ref, mate_ref, away_ref, hold_ref)
        dsec_ref[...] = dacc_ref[...]

    dwin = nn(second_t_ref[...], gup).astype(BF16)
    half = dwin.shape[0] // 2
    win_keep_ref[...] = dwin[:half]
    win_send_ref[...] = dwin[half:]


def mid_kernel(
    x_ref, attn_ref, gains_ref, dsec_ref, glow_ref, ctx_a_ref, ctx_b_ref, perm_ref, w_ref,
    gmd_ref, g2_ref, dctx_ref, keep_ref, send_ref,
):
    middle = x_ref[...].astype(F32) + attn_ref[...]
    r2 = lax.rsqrt(jnp.mean(middle * middle, axis=-1, keepdims=True) + EPS)
    normed = middle * r2
    dsec = dsec_ref[...]
    g2_ref[...] = jnp.sum(dsec * normed, axis=0, keepdims=True)
    scaled = dsec * gains_ref[1:]
    gmd = r2 * (scaled - normed * jnp.mean(scaled * normed, axis=-1, keepdims=True))
    gmd_ref[...] = gmd
    low = (glow_ref[...].astype(F32) + gmd).astype(BF16)
    dctx_ref[...] = times_transposed(low, w_ref, 0, low.shape[1]).astype(BF16)
    ctx_t = nt(perm_ref[...], jnp.concatenate([ctx_a_ref[...], ctx_b_ref[...]], axis=1)).astype(BF16)
    dw = nn(ctx_t, low).astype(BF16)
    half = dw.shape[0] // 2
    keep_ref[...] = dw[:half]
    send_ref[...] = dw[half:]


def back_kernel(q_ref, k_ref, v_ref, dctx_ref, ctx_ref, probs_ref, dq_ref, dk_ref, dv_ref, sums_ref, ds_ref, dp_ref, near_ref):
    length = q_ref.shape[0]
    tiles = length // TILE
    q, k, v, dctx = q_ref[...], k_ref[...], v_ref[...], dctx_ref[...]
    lane = lax.broadcasted_iota(jnp.int32, (length, TILE), 1)
    product = dctx.astype(F32) * ctx_ref[...].astype(F32)
    square = lambda axis: lax.broadcasted_iota(jnp.int32, (TILE, TILE), axis)
    turn = (square(0) + square(1) == TILE - 1).astype(F32)
    row = lax.broadcasted_iota(jnp.int32, (TILE, 3 * TILE), 0)
    column = lax.broadcasted_iota(jnp.int32, (TILE, 3 * TILE), 1)
    dqs, dk, dv = [], None, None

    def put(old, new):
        return new if old is None else old + new

    masked = []
    for h in range(2):
        mine = (lane < HEAD_DIM) if h == 0 else (lane >= HEAD_DIM)
        do = jnp.where(mine, dctx, jnp.zeros_like(dctx))
        dp_ref[h] = nt(do, v)
        masked.append((mine, do))
    for h in range(2):
        mine, do = masked[h]
        delta = jnp.sum(jnp.where(mine, product, 0.0), axis=-1, keepdims=True)
        far = [None, None]
        for start in range(0, TILE, CHUNK):
            band = [None, None, None]
            for t in range(tiles):
                rows = slice(t * TILE + start, t * TILE + start + CHUNK)
                ds = probs_ref[h, rows, :].astype(F32) * (dp_ref[h, rows, :] - delta[rows])
                ds_ref[h, rows, :] = ds.astype(BF16)
                for u in range(tiles):
                    d = u - t
                    part = ds[:, u * TILE : (u + 1) * TILE]
                    if abs(d) <= 1:
                        band[d + 1] = put(band[d + 1], part)
                    else:
                        far[int(d > 0)] = put(far[int(d > 0)], part)
            near_ref[start : start + CHUNK, :] = jnp.concatenate(band, axis=1)
        near = near_ref[...]
        outside = jnp.where(column < row, near, 0.0)
        near = jnp.where(column < row, 0.0, near)
        near = lax.dot_general(turn, near, (((1,), (0,)), ((), ())), precision=HIGHEST, preferred_element_type=F32)
        near = pltpu.roll(near, 0, 1, stride=1, stride_axis=0)
        sums_ref[0, h : h + 1, :] = jnp.sum(near, axis=0, keepdims=True)
        sums_ref[0, 2 + h : 3 + h, :] = jnp.sum(outside, axis=0, keepdims=True)
        for i in range(2):
            sums_ref[0, 4 + 2 * i + h : 5 + 2 * i + h, :TILE] = jnp.sum(far[i], axis=0, keepdims=True)
            sums_ref[0, 4 + 2 * i + h : 5 + 2 * i + h, TILE:] = jnp.zeros((1, 2 * TILE), F32)
        dqs.append(nn(ds_ref[h], k))
        dk = put(dk, tn(ds_ref[h], jnp.where(mine, q, jnp.zeros_like(q))))
        dv = put(dv, tn(probs_ref[h], do))
    dq_ref[...] = jnp.where(lane < HEAD_DIM, dqs[0], dqs[1]).astype(BF16)
    dk_ref[...] = dk.astype(BF16)
    dv_ref[...] = dv.astype(BF16)


def grad_kernel(dqa_ref, dqb_ref, dka_ref, dkb_ref, dva_ref, dvb_ref, first_t_ref, keep_ref, send_ref):
    refs = (dqa_ref, dqb_ref, dka_ref, dkb_ref, dva_ref, dvb_ref)
    dw = nn(first_t_ref[...], jnp.concatenate([ref[...] for ref in refs], axis=1)).astype(BF16)
    half = dw.shape[0] // 2
    keep_ref[...] = dw[:half]
    send_ref[...] = dw[half:]


def first_kernel(
    where, x_ref, gains_ref, dqa_ref, dqb_ref, dka_ref, dkb_ref, dva_ref, dvb_ref, w_ref, gmd_ref,
    g2_ref, sums_a_ref, sums_b_ref, row_keep_ref, row_mate_ref, row_away_ref, small_ref, hold_ref,
):
    width = x_ref.shape[1]
    x = x_ref[...].astype(F32)
    r1 = lax.rsqrt(jnp.mean(x * x, axis=-1, keepdims=True) + EPS)
    normed = x * r1
    refs = (dqa_ref, dqb_ref, dka_ref, dkb_ref, dva_ref, dvb_ref)
    dfirst = times_transposed(jnp.concatenate([ref[...] for ref in refs], axis=1), w_ref, 0, 3 * width)
    lines = width // TILE
    for i, gain_grad in enumerate((jnp.sum(dfirst * normed, axis=0, keepdims=True), g2_ref[...])):
        for k in range(lines):
            small_ref[i * lines + k : i * lines + k + 1, :] = gain_grad[:, k * TILE : (k + 1) * TILE]
    picked = [[], [], []]
    for ref in (sums_a_ref, sums_b_ref):
        for p in range(ref.shape[0]):
            picked[0].append(ref[p, 0:2])
            picked[1].append(ref[p, 2:4] + ref[p, 4:6])
            picked[2].append(ref[p, 6:8])
    near, below, above = (jnp.concatenate(part, axis=0) for part in picked)
    square = (3 * TILE, TILE)
    offset = lax.broadcasted_iota(jnp.int32, square, 0) - (TILE - 1)
    offset = jnp.where(offset < 0, offset + 3 * TILE, offset) - TILE
    bucket = lax.broadcasted_iota(jnp.int32, square, 1)
    choice = (bucket_of(offset) == bucket).astype(F32)
    table = lax.dot_general(near, choice, (((1,), (0,)), ((), ())), precision=HIGHEST, preferred_element_type=F32)
    lane = lax.broadcasted_iota(jnp.int32, table.shape, 1)
    table = table + jnp.where(lane == 15, jnp.sum(below, axis=-1, keepdims=True), 0.0)
    table = table + jnp.where(lane == 31, jnp.sum(above, axis=-1, keepdims=True), 0.0)
    small_ref[2 * lines : 2 * lines + HEADS, :] = table
    scaled = dfirst * gains_ref[:1]
    delta = gmd_ref[...] + r1 * (scaled - normed * jnp.mean(scaled * normed, axis=-1, keepdims=True))
    place_rows(where, delta, row_keep_ref, row_mate_ref, row_away_ref, hold_ref)


def shape(dims, dtype):
    return jax.ShapeDtypeStruct(tuple(dims), dtype)


def after(value, *earlier):
    return lax.optimization_barrier((value,) + earlier)[0]


def total(*parts):
    sums = parts[0].astype(F32)
    for part in parts[1:]:
        sums = sums + part.astype(F32)
    return sums


def on_device(
    nb, ns, hidden_in, doc_lengths, bias_table, gain_attn, gain_ffn,
    w_query, w_key, w_value, w_out, w_in, w_down, out_grad,
):
    rows_dev, shard_len, width = hidden_in.shape
    length = ns * shard_len
    ff = w_in.shape[1]
    shard = w_query.shape[0]
    b, s = lax.axis_index("batch"), lax.axis_index("seq")
    y, c = s // 2, s % 2
    bits = [1 << i for i in range(1, nb.bit_length() - 1)]
    gather_order = ([1] + bits[::-1], bits[::-1] + [1])

    def masks(core):
        value = [0]
        for bit in gather_order[core]:
            value = value + [old ^ bit for old in value]
        return value

    where = jnp.concatenate([jnp.stack([b, s]), jnp.array(masks(0) + masks(1))]).astype(jnp.int32)

    def move(value, first, second=None):
        pairs = []
        for i in range(nb):
            for j in range(ns):
                bm, sm = second if second is not None and j % 2 else first
                pairs.append((i * ns + j, (i ^ bm) * ns + (j ^ sm)))
        return lax.ppermute(value, ("batch", "seq"), pairs)

    core = lambda value: move(value, (0, 1))
    other_y = lambda value: move(value, (0, 2))

    def piece(weight, parts, axis=1):
        size = weight.shape[axis] // parts
        return lax.dynamic_slice_in_dim(weight, (c if parts == 2 else s) * size, size, axis)[None]

    def step(block, i):
        return move(block, (gather_order[0][i], 0), (gather_order[1][i], 0))

    tiled = (shard // 2) % 16 == 0

    def plain(local, pieces, axis=1, low=0, high=None):
        parts = 4 if any(entry[1] > 1 for entry in pieces) else 2
        own = jnp.stack(jnp.split(local, parts, axis))
        full = jnp.zeros((parts, nb) + own.shape[1:], BF16).at[:, b].set(own)
        for array, flip, base in pieces:
            part = s ^ flip if parts == 4 else (s ^ flip) % 2
            shards = b ^ jnp.where((s ^ flip) % 2 == 0, jnp.array(masks(0)), jnp.array(masks(1)))
            full = full.at[part, shards[base : base + array.shape[0]]].set(array[:, low:high])
        if axis == 0:
            return jnp.swapaxes(full, 0, 1)
        return full.reshape(parts, 1, -1, own.shape[2])

    class Gather:
        def __init__(self, block):
            self.block, self.brought = block, []

        def start(self):
            self.brought.append(step(self.block, len(self.brought)))
            return self.brought[-1]

        def grow(self, *gates):
            self.brought[-1] = after(self.brought[-1], *gates) if gates else self.brought[-1]
            self.block = jnp.concatenate([self.block, self.brought[-1]])
            return self.block

    vmem = pl.BlockSpec(memory_space=pltpu.VMEM)
    smem = pl.BlockSpec(memory_space=pltpu.SMEM)
    stages = len(bits) + 1

    per = width // (nb * ns)
    feature = jnp.arange(width)
    fb, fs, fr = feature // (per * ns), feature // per % ns, feature % per
    b_rel, s_rel = fb ^ b, fs ^ s
    x_rel, y_rel = b_rel % 2, s_rel // 2
    swapped = fs % 2 == 1
    position = (s_rel % 2) * 2 + jnp.where(swapped, y_rel, x_rel)
    position = position * 2 + jnp.where(swapped, x_rel, y_rel)
    for bit in bits:
        position = position * 2 + (b_rel & bit) // bit
    position = (position * per + fr).reshape(1, width)

    own = jnp.zeros((2, width), BF16)
    own = lax.dynamic_update_slice(own, jnp.stack([gain_attn, gain_ffn]), (0, b * shard)).reshape(-1, TILE)
    own = jnp.pad(own, ((0, shard - own.shape[0]), (0, TILE)))
    local1 = jnp.concatenate([w_query, w_key, w_value, own], axis=1)
    one = Gather(piece(local1, 4))
    one.start()
    row_shapes = (shape((shard_len, width), BF16),) * 2 + (shape((2, shard_len, width), BF16),)
    row_keep, row_mate, row_away, grad_keep, grad_mate, grad_away = pl.pallas_call(
        pack_kernel,
        name="pack",
        out_shape=row_shapes * 2,
        in_specs=[smem, vmem, vmem],
        cost_estimate=cost(0.9),
        compiler_params=params(),
    )(where, hidden_in, out_grad)
    row_got = other_y(row_away)
    band, seg_queries, seg_keys, perm = pl.pallas_call(
        prepare_kernel,
        name="prepare",
        out_shape=(
            shape((HEADS, TILE, 3 * TILE), F32), shape((length, TILE), BF16), shape((length, TILE), BF16),
            shape((width, width), BF16),
        ),
        in_specs=[smem, smem, smem, vmem],
        cost_estimate=cost(1.8),
        compiler_params=params(),
    )(where, doc_lengths, bias_table, position)
    def tagged(arrays, flip):
        return [(array, flip, 1 << i) for i, array in enumerate(arrays)]

    y_one = [other_y(one.brought[0])]
    while len(one.brought) < stages - 1:
        one.grow()
        one.start()
        if len(one.brought) < stages - 1:
            y_one.append(other_y(one.brought[-1]))
    one.grow(band, row_got, *y_one)
    one.start()
    y_one.append(other_y(one.brought[-2]))
    core_one = [core(array) for array in one.brought[:-1]]
    two = Gather(piece(after(w_in, one.block), 4))
    four = Gather(piece(after(w_out, one.block), 2))
    four.start()
    two.start()
    one.brought[-1] = after(one.brought[-1], *y_one, *core_one)
    core_one.append(core(one.brought[-1]))
    y_one.append(after(other_y(one.brought[-1]), two.brought[0], four.brought[0]))
    row_mate, row_far = core(row_mate), core(row_got[1])
    while len(two.brought) < stages - 1:
        two.grow()
        two.start()
    two.grow()
    y_two = [other_y(after(array, y_one[-1])) for array in two.brought]
    two.start()
    while len(four.brought) < stages:
        four.grow()
        four.start()
    three = Gather(piece(after(w_down, two.block), 2, 0))
    three.start()
    gather1 = tagged(one.brought, 0) + tagged(core_one, 1) + tagged(y_one, 2) + tagged([core(array) for array in y_one], 3)
    part = ff // 4

    row_block = shape((4, shard_len, width), BF16)
    w1_shape = shape((4, nb) + one.block.shape[1:], BF16)
    pieces1 = [local1] + [entry[0] for entry in gather1] if tiled else [plain(local1, gather1)]
    outputs = pl.pallas_call(
        functools.partial(qkv_kernel, [entry[1:] for entry in gather1] if tiled else None, shard),
        name="qkv",
        out_shape=(
            shape((length, 3 * width), BF16), shape((width, length), BF16), row_block, shape((2, width), F32),
            *([w1_shape] if tiled else []),
        ),
        in_specs=[smem] + [vmem] * (5 + len(pieces1)),
        cost_estimate=cost(2.7),
        compiler_params=params(),
    )(where, row_keep, row_mate, row_got, row_far, perm, after(pieces1[0], two.block, three.block, *four.brought), *pieces1[1:])
    qkv, first_t, xb, gains = outputs[:4]
    w1 = outputs[4] if tiled else pieces1[0]
    xb = xb.reshape(length, width)

    two.brought[-1] = after(two.brought[-1], qkv)
    y_two.append(other_y(two.brought[-1]))
    grad_got = other_y(after(grad_away, two.brought[-1]))
    while len(three.brought) < stages - 2:
        three.grow(qkv)
        three.start()
    three.grow(qkv)

    pairs = HEADS // 4
    pair_block = lambda first: pl.BlockSpec((length, TILE), lambda p: (0, first + p))
    head_block = lambda first, *dims: pl.BlockSpec((2,) + dims, lambda p: (first + p,) + (0,) * len(dims))
    whole_block = lambda *dims: pl.BlockSpec(dims, lambda p: (0,) * len(dims))

    def attend(i, gated):
        return pl.pallas_call(
            functools.partial(attention_kernel, i * pairs),
            name="attention",
            grid=(pairs,),
            out_shape=(shape((HEADS // 2, length, length), BF16), shape((length, width // 2), BF16)),
            in_specs=[
                pair_block(i * pairs), pair_block((2 + i) * pairs), pair_block((4 + i) * pairs),
                head_block(i * pairs, TILE, 3 * TILE), smem, whole_block(length, TILE), whole_block(length, TILE),
            ],
            out_specs=(head_block(0, length, length), pair_block(0)),
            scratch_shapes=[pltpu.VMEM((2, length, length), F32)],
            cost_estimate=cost(3),
            compiler_params=params(),
        )(qkv, qkv, qkv, gated, bias_table, seg_queries, seg_keys)

    probs_a, ctx_a = attend(0, after(band, two.brought[-1], three.block, *y_two[:-1]))
    probs_b, ctx_b = attend(1, after(band, ctx_a))
    three.start()
    gather4 = tagged(four.brought, 0) + tagged([core(array) for array in four.brought], 1)
    wo_shape = (2, nb, shard, width // 2)
    wo_pieces = [w_out] + [entry[0] for entry in gather4] if tiled else [plain(w_out, gather4)]
    outputs = pl.pallas_call(
        functools.partial(out_kernel, [entry[1:] for entry in gather4] if tiled else None),
        name="out",
        out_shape=(
            shape((length, width), F32), shape((length, width), BF16), shape((width, length), BF16),
            *([shape(wo_shape, BF16)] if tiled else []),
        ),
        in_specs=[smem] + [vmem] * (5 + len(wo_pieces)),
        cost_estimate=cost(1.8),
        compiler_params=params(),
    )(where, xb, ctx_a, ctx_b, gains, perm, *wo_pieces)
    attn, second, second_t = outputs[:3]
    wo = outputs[3] if tiled else wo_pieces[0]
    three.grow(second)
    high3 = three.start()
    y_two[-1] = after(y_two[-1], second)
    y_two_core = [core(after(array, ctx_b)) for array in y_two]
    gather2 = tagged(two.brought, 0) + tagged([core(array) for array in two.brought], 1) + tagged(y_two, 2) + tagged(y_two_core, 3)
    pattern2 = [entry[1:] for entry in gather2]
    arrays2 = [entry[0] for entry in gather2]
    grad_got = after(grad_got, second)
    grad_mate, grad_far = core(after(grad_mate, ctx_b)), core(grad_got[1])
    gather3 = tagged(three.brought, 0) + tagged([core(array) for array in three.brought], 1)

    steps = 4
    per_down = ff // (nb * ns)
    aligned = nb == 2 * steps and per_down % 16 == 0
    if aligned:

        def wd_index(j, place):
            rel = j ^ place[0]
            return 0, 0, rel % 2, rel // 2, 0, 0

        wd_block = pl.BlockSpec((2, 2, 1, 1, per_down, width), wd_index)
        wd_shape = shape((2, 2, 2, 2, per_down, width), BF16)
        wd_shapes, wd_blocks = (wd_shape, wd_shape), (wd_block, wd_block)
    else:
        wd_shapes = (shape((ff, width), BF16), shape((8, TILE), BF16))
        wd_blocks = (
            pl.BlockSpec((part, width), lambda j, place: (j, 0)),
            pl.BlockSpec((8, TILE), lambda j, place: (0, 0)),
        )
    place = jnp.stack([b // 2, b % 2, y, c]).astype(jnp.int32)
    full = lambda *dims: pl.BlockSpec(dims, lambda j, *place: (0,) * len(dims))
    row_specs = (full(shard_len, width), full(shard_len, width), full(2, shard_len, width))
    half = width // 2
    column_block = lambda r: pl.BlockSpec((r, part), lambda j, *place: (0, j))
    win_shape = (4, nb, shard, part)
    pieces2 = [w_in] + arrays2 if tiled else [plain(w_in, gather2, 1, 0, shard)]
    win_shape = win_shape if tiled else pieces2[0].shape
    win_block = pl.BlockSpec((1,) + win_shape[1:], lambda j, *place: (j, 0, 0, 0))
    always = lambda array: pl.BlockSpec(array.shape, lambda j, *place: (0,) * array.ndim)
    outputs = pl.pallas_call(
        functools.partial(up_kernel, pattern2 if tiled else None),
        name="up",
        out_shape=(
            shape((length, ff), BF16), shape((length, ff), BF16), *wd_shapes, *([shape(win_shape, BF16)] if tiled else []), row_block,
        ),
        grid_spec=pltpu.PrefetchScalarGridSpec(
            num_scalar_prefetch=1,
            grid=(steps,),
            in_specs=[smem, full(length, width), *row_specs[:2], row_specs[2], row_specs[0]]
            + ([always(array) for array in pieces2] if tiled else [win_block]),
            out_specs=(
                column_block(length), column_block(length), *wd_blocks, *([full(*win_shape)] if tiled else []), full(*row_block.shape),
            ),
        ),
        cost_estimate=cost(10),
        compiler_params=params(),
    )(place, where, after(second, three.block), grad_keep, grad_mate, grad_got, grad_far, *pieces2)
    act, slope, wd_keep, wd_send = outputs[:4]
    win = outputs[4] if tiled else pieces2[0]
    glow = outputs[-1].reshape(length, width)

    scatter_masks = [((1, 0), (0, 2)), ((0, 2), (1, 0))] + [((bit, 0), (bit, 0)) for bit in bits]

    class Scatter:
        def __init__(self, *held):
            self.held = [value if isinstance(value, tuple) else (value,) for value in held]
            self.rows = self.held[0][0].shape[0]
            self.widths = [value.shape[1] for value in self.held[0]]
            self.i = 0

        def outgoing(self):
            rows = slice(self.rows // 2, self.rows)
            groups = [total(*[value[rows] for value in group]).astype(BF16) for group in zip(*self.held)]
            self.sent = groups[0] if len(groups) == 1 else jnp.concatenate(groups, axis=1)
            return self.sent

        def send(self):
            self.got = move(self.sent, *scatter_masks[self.i])

        def take(self, *gates):
            self.i += 1
            self.rows //= 2
            got = after(self.got, *gates)
            starts = [sum(self.widths[:k]) for k in range(len(self.widths))]
            self.held.append(tuple(got[:, low : low + size] for low, size in zip(starts, self.widths)))

        def result(self):
            groups = [total(*[value[: self.rows] for value in group]) for group in zip(*self.held)]
            return groups[0] if len(groups) == 1 else groups

    if not aligned:
        blocks = wd_keep.reshape(nb, ns, per_down, width)

        def order(dest):
            index = jnp.arange(nb * 2)
            digits = [(index >> (stages - i)) % 2 for i in range(stages + 1)]
            x_bit = jnp.where(dest == 0, digits[0], digits[1])
            y_bit = jnp.where(dest == 0, digits[1], digits[0])
            shards = x_bit
            for bit, digit in zip(bits, digits[2:]):
                shards = shards + bit * digit
            return blocks[shards ^ b, 2 * (y_bit ^ y) + dest]

        wd_keep, wd_send = order(c), order(1 - c)
    wd_keep, wd_send = wd_keep.reshape(ff // 2, width), wd_send.reshape(ff // 2, width)
    down = Scatter(wd_keep, core(after(wd_send, high3)))
    down_sent = down.outgoing()
    down.send()

    pieces3 = [w_down] + [entry[0] for entry in gather3] if tiled else [plain(w_down, gather3, 0)]
    wd_dims = (nb, 2) + three.block.shape[1:]
    wd_spec = pl.BlockSpec((nb // steps,) + wd_dims[1:], lambda j: (j, 0, 0, 0))
    hold = pltpu.VMEM((4, shard_len, width), BF16)
    out_keep, out_mate, out_away, dsec, win_keep, win_send = pl.pallas_call(
        functools.partial(down_kernel, [entry[1:] for entry in gather3] if tiled else None),
        name="down",
        grid=(steps,),
        out_shape=(*row_shapes, shape((length, width), F32), shape((half, ff), BF16), shape((half, ff), BF16)),
        in_specs=[
            smem, full(width, length), full(length, width), full(length, width), column_block(length),
            column_block(length), win_block, *([always(array) for array in pieces3] if tiled else [wd_spec]),
        ],
        out_specs=(*row_specs, full(length, width), column_block(half), column_block(half)),
        scratch_shapes=[
            pltpu.VMEM((length, width), F32), pltpu.VMEM((length, width), F32), hold,
            *([pltpu.VMEM(wd_dims, BF16)] if tiled else []),
        ],
        cost_estimate=cost(15),
        compiler_params=params(),
    )(where, second_t, glow, attn, after(act, down_sent), slope, win, *pieces3)
    win_got = core(win_send)
    down.take(dsec)
    down_sent = down.outgoing()
    down.send()
    out_got = other_y(out_away)

    gmd, g2, dctx, wo_keep, wo_send = pl.pallas_call(
        mid_kernel,
        name="mid",
        out_shape=(
            shape((length, width), F32), shape((1, width), F32), shape((length, width), BF16),
            shape((half, width), BF16), shape((half, width), BF16),
        ),
        cost_estimate=cost(7),
        compiler_params=params(),
    )(xb, attn, gains, after(dsec, down_sent), glow, ctx_a, ctx_b, perm, wo)
    wo_got = core(wo_send)
    both = Scatter((win_keep, wo_keep), (after(win_got, dctx), wo_got))
    both_sent = both.outgoing()
    both.send()
    down.take(dctx)
    down_sent = down.outgoing()
    down.send()

    def back(i, gated):
        return pl.pallas_call(
            back_kernel,
            name="back",
            grid=(pairs,),
            out_shape=(*(shape((length, width // 2), BF16),) * 3, shape((pairs, 8, 3 * TILE), F32)),
            in_specs=[
                pair_block(i * pairs), pair_block((2 + i) * pairs), pair_block((4 + i) * pairs),
                pair_block(i * pairs), pair_block(0), head_block(0, length, length),
            ],
            out_specs=(*(pair_block(0),) * 3, pl.BlockSpec((1, 8, 3 * TILE), lambda p: (p, 0, 0))),
            scratch_shapes=[
                pltpu.VMEM((2, length, length), BF16), pltpu.VMEM((2, length, length), F32), pltpu.VMEM((TILE, 3 * TILE), F32),
            ],
            cost_estimate=cost(10),
            compiler_params=params(),
        )(qkv, qkv, qkv, gated, (ctx_a, ctx_b)[i], (probs_a, probs_b)[i])

    dq_a, dk_a, dv_a, sums_a = back(0, after(dctx, down_sent, both_sent))
    down.take(dq_a)
    down_sent = down.outgoing()
    down.send()
    dq_b, dk_b, dv_b, sums_b = back(1, after(dctx, down_sent))
    both.take(dq_b)
    both_sent = both.outgoing()
    both.send()

    grads = (after(dq_a, both_sent), dq_b, dk_a, dk_b, dv_a, dv_b)
    keep, send = pl.pallas_call(
        grad_kernel,
        name="grad",
        out_shape=(shape((half, 3 * width), BF16),) * 2,
        cost_estimate=cost(5),
        compiler_params=params(),
    )(*grads, first_t)
    last_got = core(send)
    both.take(send)
    both_sent = both.outgoing()
    both.send()
    last = Scatter(keep, after(last_got, both_sent))
    last_sent = last.outgoing()
    last.send()
    small_lines = 2 * width // TILE
    in_keep, in_mate, in_away, small = pl.pallas_call(
        first_kernel,
        name="first",
        out_shape=(*row_shapes, shape((small_lines + HEADS, TILE), F32)),
        in_specs=[smem] + [vmem] * 13,
        scratch_shapes=[hold],
        cost_estimate=cost(7),
        compiler_params=params(),
    )(where, xb, gains, after(grads[0], last_sent), *grads[1:], w1, gmd, g2, sums_a, sums_b)
    last.got = after(last.got, both.got)
    in_got = other_y(after(in_away, last.got))
    small = after(small, last.got)
    last.take()
    last_sent = last.outgoing()
    last.send()
    op2_sent = last_sent
    both.take(last_sent)
    while both.i < stages:
        both.outgoing()
        both.send()
        both.take()
    both.outgoing()
    both.send()

    def unpack(name, old, keep, mate, got):
        mate, far = core(after(mate, got)), core(got[1])
        return pl.pallas_call(
            unpack_kernel,
            name=name,
            out_shape=shape(old.shape, F32),
            in_specs=[smem] + [vmem] * 5,
            cost_estimate=cost(3),
            compiler_params=params(),
        )(where, old, keep, mate, got, far)

    out_hidden = unpack("out_rows", hidden_in, out_keep, out_mate, after(out_got, op2_sent))
    small = small + move(small, (0, 1))
    small = small + move(after(small, op2_sent), (1, 0))
    last.take(out_hidden, small)
    last.outgoing()
    last.send()
    both.take(last.sent)
    down.take(last.sent)
    while down.i < stages + 1:
        down.outgoing()
        down.send()
        down.take()
    input_grad = unpack("in_rows", out_grad, in_keep, in_mate, after(in_got, last.sent))
    for bit in bits[:-1]:
        small = small + move(after(small, last.sent), (bit, 0))
    small = small + move(small, (0, 2))
    last.take(input_grad, small)
    last_sent = last.outgoing()
    last.send()
    small = small + move(after(small, last_sent), (bits[-1], 0))
    last.take()
    while last.i < stages + 1:
        last.outgoing()
        last.send()
        last.take()
    down_grad_w = down.result()
    both_sum, last_sum = both.result(), last.result()
    gain_grads = small[:small_lines].reshape(2, width)
    gain_grads = lax.dynamic_slice_in_dim(gain_grads, (b * ns + s) * per, per, 1)
    table = small[small_lines:, :BUCKETS].T

    return (
        out_hidden,
        input_grad,
        table,
        gain_grads[0],
        gain_grads[1],
        last_sum[:, :width],
        last_sum[:, width : 2 * width],
        last_sum[:, 2 * width :],
        both_sum[1],
        both_sum[0],
        down_grad_w,
    )


def solution(mesh):
    nb, ns = mesh.shape["batch"], mesh.shape["seq"]
    placed = (
        P("batch", "seq", None),
        P("batch", None),
        P(),
        P("batch"),
        P("batch"),
        P("batch", None),
        P("batch", None),
        P("batch", None),
        P("batch", None),
        P("batch", None),
        P("batch", None),
        P("batch", "seq", None),
    )
    both = ("batch", "seq")
    return jax.shard_map(
        functools.partial(on_device, nb, ns),
        mesh=mesh,
        in_specs=placed,
        out_specs=(
            P("batch", "seq", None),
            P("batch", "seq", None),
            P(),
            P(both),
            P(both),
            P(both, None),
            P(both, None),
            P(both, None),
            P(both, None),
            P(both, None),
            P(both, None),
        ),
        check_vma=False,
    )
```
